128 devices in a mesh: fac: 8 (over y, core), jac: 16 (over x, z).
Axes of the slice: x: 4, y: 4, z: 4, core: 2. Of those that a mesh axis runs over, the one named last changes fastest.
Arguments:
- statistics: float32 [8, 2048, 2048], P(None, ('fac', 'jac')), may hold values from -24 to 24, as said below
- assignment: int32 [8], replicated, may hold values from 0 to 7, each once
Outputs:
- rotated_factor: float32 [8, 2048, 2048], P('fac', None, 'jac')
- eigen_basis: float32 [8, 2048, 2048], P('fac', None, 'jac')
The draws below stay inside these ranges and needn't reach their ends.
Inputs may be any that keep to these rules, and one draw needn't show every extreme that they name: `statistics`: each factor is symmetric. assignment is a permutation: each group takes one factor.
All inputs are finite; a program needn't handle non-finite values.
Results may differ from the reference program's by a relative error of at most 0.0025.
Values sent between devices are 32-bit elements; how exact they have to be, the bound alone decides.
No kernel may reach another device: no remote copies, remote signals or barrier semaphores. Data moves between devices by JAX's collectives and lax.ppermute only.
A program may use at most 128 MiB of HBM per device.

```python
import math
import jax
import jax.numpy as jnp
from jax import lax

BLK = 64
ROUNDS = 3
SECTIONS = 16
N = 2048
FACTORS = 8
N_JAC = 16


def draw_statistics(key, part):
    key = jax.random.fold_in(key, 11)
    key_noise, key_diag, key_scale, key_vec, key_str = jax.random.split(key, 5)
    base = jnp.clip(jax.random.normal(key_noise, (FACTORS, N, N), jnp.float32), -4.0, 4.0)
    scales = jnp.exp(jax.random.uniform(key_scale, (FACTORS, N), jnp.float32, math.log(0.7), math.log(1.4)))
    vectors = jnp.clip(jax.random.normal(key_vec, (FACTORS, 3, N), jnp.float32), -3.0, 3.0)
    strengths = jnp.exp(jax.random.uniform(key_str, (FACTORS, 3), jnp.float32, 0.0, math.log(3.0))) * (1.0 / math.sqrt(N))
    noise = (base + jnp.transpose(base, (0, 2, 1))) * (0.8 / math.sqrt(N))
    diag = jnp.exp(jax.random.uniform(key_diag, (FACTORS, N), jnp.float32, math.log(0.25), math.log(2.0)))
    eye = jnp.eye(N, dtype=jnp.float32)
    matrix = noise * (1.0 - eye) + eye * diag[:, :, None]
    for index in range(3):
        column = vectors[:, index, :]
        matrix = matrix + strengths[:, index, None, None] * column[:, :, None] * column[:, None, :]
    return matrix * scales[:, :, None] * scales[:, None, :]


def setup_inputs(seed: int = 0) -> dict:
    keys = jax.random.split(jax.random.key(seed), 3)
    return {
        "statistics": draw_statistics(jax.random.fold_in(keys[2], 71), 0),
        "assignment": jax.random.permutation(keys[1], FACTORS).astype(jnp.int32),
    }


HIGH = lax.Precision.HIGHEST

def angles(alpha, beta, gamma):
    diff = beta - alpha
    radius = jnp.sqrt(diff * diff + 4.0 * gamma * gamma)
    denom = radius * (jnp.abs(diff) + radius)
    safe = jnp.where(denom > 0, denom, 1.0)
    tangent = jnp.where(denom > 0, 2.0 * gamma * diff / safe, 0.0)
    cosine = 1.0 / jnp.sqrt(1.0 + tangent * tangent)
    return (cosine, tangent * cosine)

def turn(matrix, cosine, sine, shift):
    upper = matrix[..., :BLK]
    rolled = jnp.roll(matrix[..., BLK:], -shift, axis=-1)
    new_up = cosine * upper - sine * rolled
    new_low = sine * upper + cosine * rolled
    return jnp.concatenate([new_up, jnp.roll(new_low, shift, axis=-1)], axis=-1)

def pair_rotations(gram):
    rotation = jnp.broadcast_to(jnp.eye(2 * BLK, dtype=jnp.float32), gram.shape)
    for section in range(SECTIONS):
        diag = jnp.diagonal(gram, axis1=1, axis2=2)
        alpha = diag[:, :BLK]
        beta = jnp.roll(diag[:, BLK:], -section, axis=1)
        gamma = jnp.diagonal(jnp.roll(gram[:, :BLK, BLK:], -section, axis=2), axis1=1, axis2=2)
        cosine, sine = angles(alpha, beta, gamma)
        cosine = cosine[:, None, :]
        sine = sine[:, None, :]
        gram = turn(gram, cosine, sine, section)
        gram = jnp.transpose(turn(jnp.transpose(gram, (0, 2, 1)), cosine, sine, section), (0, 2, 1))
        rotation = turn(rotation, cosine, sine, section)
    return rotation

def move_blocks(stacked):
    upper = stacked[..., :BLK]
    lower = stacked[..., BLK:]
    new_up = jnp.concatenate([upper[0:1], lower[0:1], upper[1:N_JAC - 1]], axis=0)
    new_low = jnp.concatenate([lower[1:], upper[N_JAC - 1:]], axis=0)
    return jnp.concatenate([new_up, new_low], axis=-1)

def refresh(factor):
    stacked = jnp.transpose(factor.reshape(N, N_JAC, 2 * BLK), (1, 0, 2))
    basis = jnp.transpose(jnp.eye(N, dtype=jnp.float32).reshape(N, N_JAC, 2 * BLK), (1, 0, 2))
    for round_index in range(ROUNDS):
        gram = jnp.einsum('pri,prk->pik', stacked, stacked, precision=HIGH, preferred_element_type=jnp.float32)
        rotation = pair_rotations(gram)
        stacked = jnp.einsum('pri,pik->prk', stacked, rotation, precision=HIGH, preferred_element_type=jnp.float32)
        basis = jnp.einsum('pri,pik->prk', basis, rotation, precision=HIGH, preferred_element_type=jnp.float32)
        stacked = move_blocks(stacked)
        basis = move_blocks(basis)
    result = jnp.transpose(stacked, (1, 0, 2)).reshape(N, N)
    basis = jnp.transpose(basis, (1, 0, 2)).reshape(N, N)
    return (result, basis)

def reference(statistics, assignment):
    owner = jnp.argsort(assignment).astype(jnp.int32)
    ordered = statistics[owner]
    rotated_factor, eigen_basis = lax.map(refresh, ordered)
    return (rotated_factor, eigen_basis)
```

```python
import functools

import jax
import jax.numpy as jnp
import numpy as np
from jax import lax
from jax.experimental import pallas as pl
from jax.experimental.pallas import tpu as pltpu
from jax.sharding import PartitionSpec as P

ROUNDS = 3
HIGH = lax.Precision.HIGHEST
BLK = 64
WIDTH = 2 * BLK
SECTIONS = 16
SUB = 8
GROUPS = BLK // SUB


def lane_ids(rows):
    return lax.broadcasted_iota(jnp.int32, (rows, WIDTH), 1)


def angles(alpha, beta, gamma):
    diff = beta - alpha
    square = diff * diff + 4.0 * gamma * gamma
    turns = square > 0
    inverse = jnp.where(turns, lax.rsqrt(jnp.where(turns, square, 1.0)), 0.0)
    along = diff * inverse
    lead = 1.0 + jnp.abs(along)
    cross = 2.0 * gamma * inverse * along
    scale = lax.rsqrt(lead * lead + cross * cross)
    return lead * scale, cross * scale


def small_rotation(gram, store):
    lanes = lane_ids(WIDTH)
    rows = lax.broadcasted_iota(jnp.int32, (WIDTH, WIDTH), 0)
    upper_half = lanes & BLK
    skew = ((rows - lanes) & (BLK - 1)) + upper_half
    store[...] = jnp.take_along_axis(gram, skew, axis=1).T
    low = lane_ids(SUB) < BLK
    aa, bb, tt, dd = [], [], [], []
    for b in range(GROUPS):
        top = store[pl.ds(b, SUB, stride=SUB), :]
        bot = store[pl.ds(BLK + b, SUB, stride=SUB), :]
        top_swap = pltpu.roll(top, BLK, 1)
        bot_swap = pltpu.roll(bot, BLK, 1)
        aa.append(jnp.where(low, top, top_swap))
        tt.append(jnp.where(low, top_swap, top))
        bb.append(jnp.where(low, bot, bot_swap))
        dd.append(jnp.where(low, bot_swap, bot))
    first_rows = lax.broadcasted_iota(jnp.int32, (SUB, WIDTH), 0)
    start = jnp.where(first_rows == 0, 1.0, 0.0).astype(jnp.float32)
    zero = jnp.zeros((SUB, WIDTH), jnp.float32)
    ru = [jnp.where(low, start, 0.0)] + [zero] * (GROUPS - 1)
    rl = [jnp.where(low, 0.0, start)] + [zero] * (GROUPS - 1)

    def spread(x, row):
        return jnp.broadcast_to(x[row:row + 1], (SUB, WIDTH))

    alpha, beta, gamma = spread(aa[0], 0), spread(dd[0], 0), spread(bb[0], 0)
    for section in range(SECTIONS):
        c, s = angles(alpha, beta, gamma)
        cc = [pltpu.roll(c, b, 1, stride=SUB, stride_axis=0) for b in range(GROUPS)]
        ss = [pltpu.roll(s, b, 1, stride=SUB, stride_axis=0) for b in range(GROUPS)]
        new_ru = [cc[b] * ru[b] - ss[b] * rl[b] for b in range(GROUPS)]
        new_rl = [ss[b] * ru[b] + cc[b] * rl[b] for b in range(GROUPS)]
        ru, rl = new_ru, new_rl
        if section == SECTIONS - 1:
            break
        rl = [pltpu.roll(rl[-1], 1, 0)] + rl[:-1]
        a1 = [cc[b] * aa[b] - ss[b] * bb[b] for b in range(GROUPS)]
        b1 = [ss[b] * aa[b] + cc[b] * bb[b] for b in range(GROUPS)]
        t1 = [cc[b] * tt[b] - ss[b] * dd[b] for b in range(GROUPS)]
        d1 = [ss[b] * tt[b] + cc[b] * dd[b] for b in range(GROUPS)]
        aa = [c * a1[b] - s * t1[b] for b in range(GROUPS)]
        t2 = [s * a1[b] + c * t1[b] for b in range(GROUPS)]
        b2 = [c * b1[b] - s * d1[b] for b in range(GROUPS)]
        d2 = [s * b1[b] + c * d1[b] for b in range(GROUPS)]
        new_alpha = c * (c * alpha - s * gamma) - s * (c * gamma - s * beta)
        new_beta = s * (s * alpha + c * gamma) + c * (s * gamma + c * beta)
        alpha, beta = new_alpha, pltpu.roll(new_beta, WIDTH - 1, 1)
        gamma = spread(b2[-1], SUB - 1)
        bb = [pltpu.roll(b2[-1], 1, 0)] + b2[:-1]
        t2 = t2[1:] + [pltpu.roll(t2[0], SUB - 1, 0)]
        tt = [pltpu.roll(x, WIDTH - 1, 1) for x in t2]
        dd = [pltpu.roll(x, WIDTH - 1, 1) for x in d2]
    for b in range(GROUPS):
        store[pl.ds(b, SUB, stride=SUB), :] = ru[b]
        store[pl.ds(BLK + b, SUB, stride=SUB), :] = rl[b]
    offset = jnp.where(upper_half == 0, 0, SECTIONS - 1)
    unskew = ((rows - lanes + offset) & (BLK - 1)) + upper_half
    return jnp.take_along_axis(store[...].T, unskew, axis=1)


def deal_kernel(assignment, stats, out):
    factors, _, order = stats.shape
    count = order // WIDTH
    for factor in range(factors):
        group = assignment[factor]
        for place in range(count):
            out[group * count + place] = stats[factor, :, place * WIDTH:(place + 1) * WIDTH]


def product(a, b):
    return jnp.dot(a, b, precision=HIGH, preferred_element_type=jnp.float32)


def post(place, turned, right, left, columns):
    top, bottom = turned[:BLK], turned[BLK:]
    first = place == 0
    right[:, columns] = jnp.where(first, bottom, top)
    left[:, columns] = jnp.where(first, top, bottom)


def first_kernel(place_ref, work, right, left, store):
    place = place_ref[0]
    order = work.shape[0]
    straight = work[...]
    flat = straight.T
    rotation = small_rotation(product(flat, straight), store).T
    post(place, product(rotation, flat), right, left, pl.ds(0, order))
    post(place, rotation, right, left, pl.ds(order, WIDTH))


def gather_pair(place, last, own_right, own_left, came_right, came_left, pair, sems):
    upper, lower = pair.at[pl.ds(0, BLK)], pair.at[pl.ds(BLK, BLK)]

    @pl.when(place == 0)
    def _():
        pltpu.make_async_copy(own_left, upper, sems.at[0]).start()

    @pl.when(place != 0)
    def _():
        pltpu.make_async_copy(came_right, upper, sems.at[0]).start()

    @pl.when(place == last)
    def _():
        pltpu.make_async_copy(own_right, lower, sems.at[1]).start()

    @pl.when(place != last)
    def _():
        pltpu.make_async_copy(came_left, lower, sems.at[1]).start()

    pltpu.make_async_copy(came_right, upper, sems.at[0]).wait()
    pltpu.make_async_copy(came_left, lower, sems.at[1]).wait()


def next_kernel(last, order, place_ref, own_right, own_left, came_right, came_left, right, left, pair, store, sems):
    place = place_ref[0]
    gather_pair(place, last, own_right, own_left, came_right, came_left, pair, sems)
    support = pair.shape[1] - order
    flat = pair[:, :order]
    gram = lax.dot_general(
        flat, flat, (((1,), (1,)), ((), ())), precision=HIGH, preferred_element_type=jnp.float32
    )
    rotation = small_rotation(gram, store).T
    post(place, product(rotation, flat), right, left, pl.ds(0, order))
    upper = product(rotation[:, :BLK], pair[:BLK, order:])
    post(place, upper, right, left, pl.ds(order, support))
    lower = product(rotation[:, BLK:], pair[BLK:, order:])
    post(place, lower, right, left, pl.ds(order + support, support))


def last_kernel(last, order, place_ref, table, own_right, own_left, came_right, came_left, work, basis, pair, sems):
    place = place_ref[0]
    gather_pair(place, last, own_right, own_left, came_right, came_left, pair, sems)
    work[...] = pair[:, :order].T
    basis[...] = jnp.zeros_like(basis)
    chunks = (pair.shape[1] - order) // WIDTH
    tops = lane_ids(WIDTH) < BLK
    for half in range(2):
        for chunk in range(chunks):
            row = pl.multiple_of(table[place, half * chunks + chunk] * WIDTH, WIDTH)
            piece = pair[:, order + chunk * WIDTH:order + (chunk + 1) * WIDTH].T
            keep = tops if half == 0 else jnp.logical_not(tops)
            basis[pl.ds(row, WIDTH), :] += jnp.where(keep, piece, 0.0)


def support_table(count):
    source_top = [max(p - 1, 0) for p in range(count)]
    source_bottom = [min(p + 1, count - 1) for p in range(count)]
    support = [[p] for p in range(count)]
    for _ in range(ROUNDS - 1):
        support = [support[source_top[p]] + support[source_bottom[p]] for p in range(count)]
    return np.array([support[source_top[p]] + support[source_bottom[p]] for p in range(count)], np.int32)


def vmem():
    return pl.BlockSpec(memory_space=pltpu.VMEM)


def smem():
    return pl.BlockSpec(memory_space=pltpu.SMEM)


def anywhere():
    return pl.BlockSpec(memory_space=pl.ANY)


PARAMS = pltpu.CompilerParams(vmem_limit_bytes=40 * 1024 * 1024)


def shape(*dims):
    return jax.ShapeDtypeStruct(dims, jnp.float32)


def shards(statistics, assignment):
    factors, slab, order = statistics.shape
    count = order // WIDTH
    devices = factors * count
    last = count - 1
    place = lax.axis_index("jac").astype(jnp.int32).reshape(1)
    dealt = pl.pallas_call(
        deal_kernel,
        out_shape=shape(devices, slab, WIDTH),
        in_specs=[smem(), vmem()],
        out_specs=vmem(),
        compiler_params=PARAMS,
        name="deal",
    )(assignment, statistics)
    moved = lax.all_to_all(dealt, ("fac", "jac"), split_axis=0, concat_axis=0, tiled=True)
    work = moved.reshape(order, WIDTH)
    support = WIDTH
    right, left = pl.pallas_call(
        first_kernel,
        out_shape=[shape(BLK, order + support)] * 2,
        in_specs=[smem(), vmem()],
        out_specs=[vmem()] * 2,
        scratch_shapes=[pltpu.VMEM((WIDTH, WIDTH), jnp.float32)],
        compiler_params=PARAMS,
        name="first_round",
    )(place, work)
    forward = [(p, p + 1) for p in range(last)]
    backward = [(p + 1, p) for p in range(last)]
    for _ in range(ROUNDS - 1):
        came_right = lax.ppermute(right, "jac", forward)
        came_left = lax.ppermute(left, "jac", backward)
        right, left = pl.pallas_call(
            functools.partial(next_kernel, last, order),
            out_shape=[shape(BLK, order + 2 * support)] * 2,
            in_specs=[smem()] + [anywhere()] * 4,
            out_specs=[vmem()] * 2,
            scratch_shapes=[
                pltpu.VMEM((WIDTH, order + support), jnp.float32),
                pltpu.VMEM((WIDTH, WIDTH), jnp.float32),
                pltpu.SemaphoreType.DMA((2,)),
            ],
            compiler_params=PARAMS,
            name="next_round",
        )(place, right, left, came_right, came_left)
        support = 2 * support
    came_right = lax.ppermute(right, "jac", forward)
    came_left = lax.ppermute(left, "jac", backward)
    work, basis = pl.pallas_call(
        functools.partial(last_kernel, last, order),
        out_shape=[shape(order, WIDTH)] * 2,
        in_specs=[smem(), smem()] + [anywhere()] * 4,
        out_specs=[vmem()] * 2,
        scratch_shapes=[
            pltpu.VMEM((WIDTH, order + support), jnp.float32),
            pltpu.SemaphoreType.DMA((2,)),
        ],
        compiler_params=PARAMS,
        name="output",
    )(place, jnp.asarray(support_table(count)), right, left, came_right, came_left)
    return work[None], basis[None]


def solution(mesh):
    return jax.shard_map(
        shards,
        mesh=mesh,
        in_specs=(P(None, ("fac", "jac"), None), P()),
        out_specs=(P("fac", None, "jac"), P("fac", None, "jac")),
        check_vma=False,
    )
```

```python
import functools

import jax
import jax.numpy as jnp
import numpy as np
from jax import lax
from jax.experimental import pallas as pl
from jax.experimental.pallas import tpu as pltpu
from jax.sharding import PartitionSpec as P

ROUNDS = 3
HIGH = lax.Precision.HIGHEST
BLK = 64
WIDTH = 2 * BLK
SECTIONS = 16
SUB = 8
GROUPS = BLK // SUB


def lane_ids(rows):
    return lax.broadcasted_iota(jnp.int32, (rows, WIDTH), 1)


def angles(alpha, beta, gamma):
    diff = beta - alpha
    square = diff * diff + 4.0 * gamma * gamma
    turns = square > 0
    inverse = jnp.where(turns, lax.rsqrt(jnp.where(turns, square, 1.0)), 0.0)
    along = diff * inverse
    lead = 1.0 + jnp.abs(along)
    cross = 2.0 * gamma * inverse * along
    scale = lax.rsqrt(lead * lead + cross * cross)
    return lead * scale, cross * scale


def small_rotation(gram, store, swapped):
    lanes = lane_ids(WIDTH)
    rows = lax.broadcasted_iota(jnp.int32, (WIDTH, WIDTH), 0)
    upper_half = lanes & BLK
    skew = ((rows - lanes) & (BLK - 1)) + upper_half
    store[...] = jnp.take_along_axis(gram, skew, axis=1).T
    low = lane_ids(SUB) < BLK
    aa, bb, tt, dd = [], [], [], []
    for b in range(GROUPS):
        top = store[pl.ds(b, SUB, stride=SUB), :]
        bot = store[pl.ds(BLK + b, SUB, stride=SUB), :]
        top_swap = pltpu.roll(top, BLK, 1)
        bot_swap = pltpu.roll(bot, BLK, 1)
        blocks = (
            jnp.where(low, top, top_swap),
            jnp.where(low, bot, bot_swap),
            jnp.where(low, top_swap, top),
            jnp.where(low, bot_swap, bot),
        )
        aa.append(jnp.where(swapped, blocks[3], blocks[0]))
        bb.append(jnp.where(swapped, blocks[2], blocks[1]))
        tt.append(jnp.where(swapped, blocks[1], blocks[2]))
        dd.append(jnp.where(swapped, blocks[0], blocks[3]))
    first_rows = lax.broadcasted_iota(jnp.int32, (SUB, WIDTH), 0)
    start = jnp.where(first_rows == 0, 1.0, 0.0).astype(jnp.float32)
    zero = jnp.zeros((SUB, WIDTH), jnp.float32)
    ru = [jnp.where(low, start, 0.0)] + [zero] * (GROUPS - 1)
    rl = [jnp.where(low, 0.0, start)] + [zero] * (GROUPS - 1)

    def spread(x, row):
        return jnp.broadcast_to(x[row:row + 1], (SUB, WIDTH))

    alpha, beta, gamma = spread(aa[0], 0), spread(dd[0], 0), spread(bb[0], 0)
    for section in range(SECTIONS):
        c, s = angles(alpha, beta, gamma)
        cc = [pltpu.roll(c, b, 1, stride=SUB, stride_axis=0) for b in range(GROUPS)]
        ss = [pltpu.roll(s, b, 1, stride=SUB, stride_axis=0) for b in range(GROUPS)]
        new_ru = [cc[b] * ru[b] - ss[b] * rl[b] for b in range(GROUPS)]
        new_rl = [ss[b] * ru[b] + cc[b] * rl[b] for b in range(GROUPS)]
        ru, rl = new_ru, new_rl
        if section == SECTIONS - 1:
            break
        rl = [pltpu.roll(rl[-1], 1, 0)] + rl[:-1]
        a1 = [cc[b] * aa[b] - ss[b] * bb[b] for b in range(GROUPS)]
        b1 = [ss[b] * aa[b] + cc[b] * bb[b] for b in range(GROUPS)]
        t1 = [cc[b] * tt[b] - ss[b] * dd[b] for b in range(GROUPS)]
        d1 = [ss[b] * tt[b] + cc[b] * dd[b] for b in range(GROUPS)]
        aa = [c * a1[b] - s * t1[b] for b in range(GROUPS)]
        t2 = [s * a1[b] + c * t1[b] for b in range(GROUPS)]
        b2 = [c * b1[b] - s * d1[b] for b in range(GROUPS)]
        d2 = [s * b1[b] + c * d1[b] for b in range(GROUPS)]
        new_alpha = c * (c * alpha - s * gamma) - s * (c * gamma - s * beta)
        new_beta = s * (s * alpha + c * gamma) + c * (s * gamma + c * beta)
        alpha, beta = new_alpha, pltpu.roll(new_beta, WIDTH - 1, 1)
        gamma = spread(b2[-1], SUB - 1)
        bb = [pltpu.roll(b2[-1], 1, 0)] + b2[:-1]
        t2 = t2[1:] + [pltpu.roll(t2[0], SUB - 1, 0)]
        tt = [pltpu.roll(x, WIDTH - 1, 1) for x in t2]
        dd = [pltpu.roll(x, WIDTH - 1, 1) for x in d2]
    for b in range(GROUPS):
        store[pl.ds(b, SUB, stride=SUB), :] = ru[b]
        store[pl.ds(BLK + b, SUB, stride=SUB), :] = rl[b]
    offset = jnp.where(upper_half == 0, 0, SECTIONS - 1)
    unskew = ((rows - lanes + offset) & (BLK - 1)) + upper_half
    return jnp.take_along_axis(store[...].T, unskew, axis=1)


def deal_kernel(assignment, home, stats, out):
    factors, _, order = stats.shape
    count = order // WIDTH
    for factor in range(factors):
        group = assignment[factor]
        for place in range(count):
            out[home[group * count + place]] = stats[factor, :, place * WIDTH:(place + 1) * WIDTH]


def product(a, b):
    return jnp.dot(a, b, precision=HIGH, preferred_element_type=jnp.float32)


def swap_halves(x, axis, swapped):
    return jnp.where(swapped, pltpu.roll(x, BLK, axis), x)


def leave_rotation(gram, store, place, swapped):
    rotation = small_rotation(gram, store, swapped).T
    bottom_first = jnp.logical_or(place == 0, place % 2 == 1)
    return swap_halves(rotation, 0, bottom_first)


def post(near, far, columns, block):
    near[:, columns] = block[:BLK]
    far[:, columns] = block[BLK:]


def first_kernel(me, places, work, near, far, store):
    place = places[me[0]]
    order = work.shape[0]
    straight = work[...]
    flat = straight.T
    rotation = leave_rotation(product(flat, straight), store, place, False)
    post(near, far, pl.ds(0, order), product(rotation, flat))
    post(near, far, pl.ds(order, WIDTH), rotation)


def next_kernel(order, me, places, from_near, from_far, near, far, store):
    place = places[me[0]]
    support = from_near.shape[1] - order
    swapped = place % 2 == 0
    flat = jnp.concatenate([from_near[:, :order], from_far[:, :order]], axis=0)
    rotation = leave_rotation(product(flat, flat.T), store, place, swapped)
    rotation = swap_halves(rotation, 1, swapped)
    post(near, far, pl.ds(0, order), product(rotation, flat))
    side, other = rotation[:, :BLK], rotation[:, BLK:]
    if support == WIDTH:
        post(near, far, pl.ds(order, WIDTH), product(side, from_near[:, order:]))
        post(near, far, pl.ds(order + WIDTH, WIDTH), product(other, from_far[:, order:]))
    else:
        shared = jnp.concatenate([from_near[:, order:order + WIDTH], from_far[:, order + WIDTH:]], axis=0)
        post(near, far, pl.ds(order, WIDTH), product(rotation, shared))
        post(near, far, pl.ds(order + WIDTH, WIDTH), product(side, from_near[:, order + WIDTH:]))
        post(near, far, pl.ds(order + 2 * WIDTH, WIDTH), product(other, from_far[:, order:order + WIDTH]))


def last_kernel(me, table, from_near, from_far, work, basis):
    order = work.shape[0]
    place = me[0] % table.shape[0]
    even = place % 2 == 0
    near, far = from_near[:, :order], from_far[:, :order]
    top, bottom = jnp.where(even, far, near), jnp.where(even, near, far)
    work[...] = jnp.concatenate([top, bottom], axis=0).T
    basis[...] = jnp.zeros_like(basis)
    chunks = (from_near.shape[1] - order) // WIDTH
    left_half = lane_ids(WIDTH) < BLK
    for chunk in range(chunks):
        columns = pl.ds(order + chunk * WIDTH, WIDTH)
        piece = jnp.concatenate([from_near[:, columns], from_far[:, columns]], axis=0).T
        piece = swap_halves(piece, 1, even)
        for half in range(2):
            row = pl.multiple_of(table[place, half * chunks + chunk] * WIDTH, WIDTH)
            left = jnp.logical_xor(even, half == 0)
            basis[pl.ds(row, WIDTH), :] += jnp.where(left_half == left, piece, 0.0)


def far_place(place, count):
    return min(max(place + (1 if place % 2 else -1), 0), count - 1)


def support_table(count):
    far = [far_place(p, count) for p in range(count)]
    second = [[p ^ 1, far[p]] for p in range(count)]
    third = [[p, second[p ^ 1][1], second[far[p]][0]] for p in range(count)]
    return np.array([third[p ^ 1] + third[far[p]] for p in range(count)], np.int32)


def homes(factors, count):
    return np.arange(factors * count, dtype=np.int32)


def vmem():
    return pl.BlockSpec(memory_space=pltpu.VMEM)


def smem():
    return pl.BlockSpec(memory_space=pltpu.SMEM)


PARAMS = pltpu.CompilerParams(vmem_limit_bytes=40 * 1024 * 1024)


def shape(*dims):
    return jax.ShapeDtypeStruct(dims, jnp.float32)


def shards(statistics, assignment):
    factors, slab, order = statistics.shape
    count = order // WIDTH
    devices = factors * count
    axes = ("fac", "jac")
    home = homes(factors, count)
    places = np.zeros(devices, np.int32)
    places[home] = np.arange(devices) % count
    me = lax.axis_index(axes).astype(jnp.int32).reshape(1)
    dealt = pl.pallas_call(
        deal_kernel,
        out_shape=shape(devices, slab, WIDTH),
        in_specs=[smem(), smem(), vmem()],
        out_specs=vmem(),
        compiler_params=PARAMS,
        name="deal",
    )(assignment, jnp.asarray(home), statistics)
    moved = lax.all_to_all(dealt, axes, split_axis=0, concat_axis=0, tiled=True)
    work = moved.reshape(order, WIDTH)
    places = jnp.asarray(places)
    store = pltpu.VMEM((WIDTH, WIDTH), jnp.float32)
    near, far = pl.pallas_call(
        first_kernel,
        out_shape=[shape(BLK, order + WIDTH)] * 2,
        in_specs=[smem(), smem(), vmem()],
        out_specs=[vmem()] * 2,
        scratch_shapes=[store],
        compiler_params=PARAMS,
        name="first_round",
    )(me, places, work)
    for later in range(1, ROUNDS + 1):
        goal = home if later < ROUNDS else np.arange(devices, dtype=np.int32)
        near_route, far_route = [], []
        for group in range(factors):
            for place in range(count):
                start = int(home[group * count + place])
                near_route.append((start, int(goal[group * count + (place ^ 1)])))
                far_route.append((start, int(goal[group * count + far_place(place, count)])))
        from_far = lax.ppermute(far, axes, far_route)
        from_near = lax.ppermute(near, axes, near_route)
        if later < ROUNDS:
            near, far = pl.pallas_call(
                functools.partial(next_kernel, order),
                out_shape=[shape(BLK, order + (later + 1) * WIDTH)] * 2,
                in_specs=[smem(), smem(), vmem(), vmem()],
                out_specs=[vmem()] * 2,
                scratch_shapes=[store],
                compiler_params=PARAMS,
                name="next_round",
            )(me, places, from_near, from_far)
    work, basis = pl.pallas_call(
        last_kernel,
        out_shape=[shape(order, WIDTH)] * 2,
        in_specs=[smem(), smem(), vmem(), vmem()],
        out_specs=[vmem()] * 2,
        compiler_params=PARAMS,
        name="output",
    )(me, jnp.asarray(support_table(count)), from_near, from_far)
    return work[None], basis[None]


def solution(mesh):
    return jax.shard_map(
        shards,
        mesh=mesh,
        in_specs=(P(None, ("fac", "jac"), None), P()),
        out_specs=(P("fac", None, "jac"), P("fac", None, "jac")),
        check_vma=False,
    )
```

```python
import functools

import jax
import jax.numpy as jnp
import numpy as np
from jax import lax
from jax.experimental import pallas as pl
from jax.experimental.pallas import tpu as pltpu
from jax.sharding import PartitionSpec as P

ROUNDS = 3
CHUNK = 512
BLK = 64
WIDTH = 2 * BLK
SECTIONS = 16
SUB = 8
GROUPS = BLK // SUB


def lane_ids(rows):
    return lax.broadcasted_iota(jnp.int32, (rows, WIDTH), 1)


def angles(alpha, beta, gamma):
    diff = beta - alpha
    square = diff * diff + 4.0 * gamma * gamma
    turns = square > 0
    inverse = jnp.where(turns, lax.rsqrt(jnp.where(turns, square, 1.0)), 0.0)
    along = diff * inverse
    lead = 1.0 + jnp.abs(along)
    cross = 2.0 * gamma * inverse * along
    scale = lax.rsqrt(lead * lead + cross * cross)
    return lead * scale, cross * scale


def small_rotation(gram, store, swapped):
    lanes = lane_ids(WIDTH)
    rows = lax.broadcasted_iota(jnp.int32, (WIDTH, WIDTH), 0)
    upper_half = lanes & BLK
    skew = ((rows - lanes) & (BLK - 1)) + upper_half
    store[...] = jnp.take_along_axis(gram, skew, axis=1).T
    low = lane_ids(SUB) < BLK
    aa, bb, tt, dd = [], [], [], []
    for b in range(GROUPS):
        top = store[pl.ds(b, SUB, stride=SUB), :]
        bot = store[pl.ds(BLK + b, SUB, stride=SUB), :]
        top_swap = pltpu.roll(top, BLK, 1)
        bot_swap = pltpu.roll(bot, BLK, 1)
        blocks = (
            jnp.where(low, top, top_swap),
            jnp.where(low, bot, bot_swap),
            jnp.where(low, top_swap, top),
            jnp.where(low, bot_swap, bot),
        )
        aa.append(jnp.where(swapped, blocks[3], blocks[0]))
        bb.append(jnp.where(swapped, blocks[2], blocks[1]))
        tt.append(jnp.where(swapped, blocks[1], blocks[2]))
        dd.append(jnp.where(swapped, blocks[0], blocks[3]))
    first_rows = lax.broadcasted_iota(jnp.int32, (SUB, WIDTH), 0)
    start = jnp.where(first_rows == 0, 1.0, 0.0).astype(jnp.float32)
    zero = jnp.zeros((SUB, WIDTH), jnp.float32)
    ru = [jnp.where(low, start, 0.0)] + [zero] * (GROUPS - 1)
    rl = [jnp.where(low, 0.0, start)] + [zero] * (GROUPS - 1)

    def spread(x, row):
        return jnp.broadcast_to(x[row:row + 1], (SUB, WIDTH))

    alpha, beta, gamma = spread(aa[0], 0), spread(dd[0], 0), spread(bb[0], 0)
    for section in range(SECTIONS):
        c, s = angles(alpha, beta, gamma)
        cc = [pltpu.roll(c, b, 1, stride=SUB, stride_axis=0) for b in range(GROUPS)]
        ss = [pltpu.roll(s, b, 1, stride=SUB, stride_axis=0) for b in range(GROUPS)]
        new_ru = [cc[b] * ru[b] - ss[b] * rl[b] for b in range(GROUPS)]
        new_rl = [ss[b] * ru[b] + cc[b] * rl[b] for b in range(GROUPS)]
        ru, rl = new_ru, new_rl
        if section == SECTIONS - 1:
            break
        rl = [pltpu.roll(rl[-1], 1, 0)] + rl[:-1]
        a1 = [cc[b] * aa[b] - ss[b] * bb[b] for b in range(GROUPS)]
        b1 = [ss[b] * aa[b] + cc[b] * bb[b] for b in range(GROUPS)]
        t1 = [cc[b] * tt[b] - ss[b] * dd[b] for b in range(GROUPS)]
        d1 = [ss[b] * tt[b] + cc[b] * dd[b] for b in range(GROUPS)]
        aa = [c * a1[b] - s * t1[b] for b in range(GROUPS)]
        t2 = [s * a1[b] + c * t1[b] for b in range(GROUPS)]
        b2 = [c * b1[b] - s * d1[b] for b in range(GROUPS)]
        d2 = [s * b1[b] + c * d1[b] for b in range(GROUPS)]
        new_alpha = c * (c * alpha - s * gamma) - s * (c * gamma - s * beta)
        new_beta = s * (s * alpha + c * gamma) + c * (s * gamma + c * beta)
        alpha, beta = new_alpha, pltpu.roll(new_beta, WIDTH - 1, 1)
        gamma = spread(b2[-1], SUB - 1)
        bb = [pltpu.roll(b2[-1], 1, 0)] + b2[:-1]
        t2 = t2[1:] + [pltpu.roll(t2[0], SUB - 1, 0)]
        tt = [pltpu.roll(x, WIDTH - 1, 1) for x in t2]
        dd = [pltpu.roll(x, WIDTH - 1, 1) for x in d2]
    for b in range(GROUPS):
        store[pl.ds(b, SUB, stride=SUB), :] = ru[b]
        store[pl.ds(BLK + b, SUB, stride=SUB), :] = rl[b]
    offset = jnp.where(upper_half == 0, 0, SECTIONS - 1)
    unskew = ((rows - lanes + offset) & (BLK - 1)) + upper_half
    return jnp.take_along_axis(store[...].T, unskew, axis=1)


def deal_kernel(assignment, home, stats, out):
    factors, _, order = stats.shape
    count = order // WIDTH
    for factor in range(factors):
        group = assignment[factor]
        for place in range(count):
            out[home[group * count + place]] = stats[factor, :, place * WIDTH:(place + 1) * WIDTH]


def pieces(x):
    high = x.astype(jnp.bfloat16)
    rest = x - high.astype(jnp.float32)
    middle = rest.astype(jnp.bfloat16)
    low = (rest - middle.astype(jnp.float32)).astype(jnp.bfloat16)
    return high, middle, low


def gram_of(parts):
    high, middle, low = parts
    left = jnp.concatenate([high, middle, low], axis=0)
    right = jnp.concatenate([high, middle], axis=0)
    full = lax.dot_general(left, right, (((1,), (1,)), ((), ())), preferred_element_type=jnp.float32)
    crossed = full[2 * WIDTH:, :WIDTH]
    small = full[WIDTH:2 * WIDTH, WIDTH:] + (crossed + crossed.T)
    return full[:WIDTH, :WIDTH] + (full[:WIDTH, WIDTH:] + full[WIDTH:2 * WIDTH, :WIDTH] + small)


def apply(rotation, parts, near, far, start, exact):
    high, middle, low = pieces(rotation)
    first = jnp.concatenate(
        [jnp.concatenate([high, middle], axis=1), jnp.concatenate([middle, high], axis=1)], axis=0
    )
    last = jnp.concatenate([low, high], axis=1)
    total = parts[0].shape[1]
    for begin in range(0, total, CHUNK):
        end = min(begin + CHUNK, total)
        part = [x[:, begin:end] for x in parts]
        both = jnp.dot(first, jnp.concatenate(part[:2], axis=0), preferred_element_type=jnp.float32)
        small = both[WIDTH:]
        if exact:
            small = small + jnp.dot(
                last, jnp.concatenate([part[0], part[2]], axis=0), preferred_element_type=jnp.float32
            )
        post(near, far, pl.ds(start + begin, end - begin), both[:WIDTH] + small)


def swap_halves(x, axis, swapped):
    return jnp.where(swapped, pltpu.roll(x, BLK, axis), x)


def leave_rotation(gram, store, place, swapped):
    rotation = small_rotation(gram, store, swapped).T
    bottom_first = jnp.logical_or(place == 0, place % 2 == 1)
    return swap_halves(rotation, 0, bottom_first)


def post(near, far, columns, block):
    near[:, columns] = block[:BLK]
    far[:, columns] = block[BLK:]


def first_kernel(me, places, work, near, far, store):
    place = places[me[0]]
    order = work.shape[0]
    parts = pieces(work[...].T)
    rotation = leave_rotation(gram_of(parts), store, place, False)
    apply(rotation, parts, near, far, 0, True)
    post(near, far, pl.ds(order, WIDTH), rotation)


def next_kernel(order, final, me, places, from_near, from_far, near, far, store):
    place = places[me[0]]
    swapped = place % 2 == 0
    parts = pieces(jnp.concatenate([from_near[:, :order], from_far[:, :order]], axis=0))
    rotation = leave_rotation(gram_of(parts), store, place, swapped)
    rotation = swap_halves(rotation, 1, swapped)
    apply(rotation, parts, near, far, 0, not final)
    blank = jnp.zeros((BLK, WIDTH), jnp.float32)
    near_basis = [from_near[:, c:c + WIDTH] for c in range(order, from_near.shape[1], WIDTH)]
    far_basis = [from_far[:, c:c + WIDTH] for c in range(order, from_far.shape[1], WIDTH)]
    if final:
        near_basis, far_basis = near_basis + [blank], [far_basis[1], blank, far_basis[0]]
    else:
        near_basis, far_basis = near_basis + [blank], [blank] + far_basis
    columns = [jnp.concatenate(halves, axis=0) for halves in zip(near_basis, far_basis)]
    apply(rotation, pieces(jnp.concatenate(columns, axis=1)), near, far, order, False)


def last_kernel(me, table, from_near, from_far, work, basis):
    order = work.shape[0]
    place = me[0] % table.shape[0]
    even = place % 2 == 0
    near, far = from_near[:, :order], from_far[:, :order]
    top, bottom = jnp.where(even, far, near), jnp.where(even, near, far)
    work[...] = jnp.concatenate([top, bottom], axis=0).T
    basis[...] = jnp.zeros_like(basis)
    chunks = (from_near.shape[1] - order) // WIDTH
    left_half = lane_ids(WIDTH) < BLK
    for chunk in range(chunks):
        columns = pl.ds(order + chunk * WIDTH, WIDTH)
        piece = jnp.concatenate([from_near[:, columns], from_far[:, columns]], axis=0).T
        piece = swap_halves(piece, 1, even)
        for half in range(2):
            row = pl.multiple_of(table[place, half * chunks + chunk] * WIDTH, WIDTH)
            left = jnp.logical_xor(even, half == 0)
            basis[pl.ds(row, WIDTH), :] += jnp.where(left_half == left, piece, 0.0)


def far_place(place, count):
    return min(max(place + (1 if place % 2 else -1), 0), count - 1)


def support_table(count):
    far = [far_place(p, count) for p in range(count)]
    second = [[p ^ 1, far[p]] for p in range(count)]
    third = [[p, second[p ^ 1][1], second[far[p]][0]] for p in range(count)]
    return np.array([third[p ^ 1] + third[far[p]] for p in range(count)], np.int32)


PAIR_Z = (((1, 0), (3, 2)), ((3, 2), (1, 0)))


def homes(factors, count):
    home = np.zeros(factors * count, np.int32)
    for group in range(factors):
        for place in range(count):
            x, pair, core = place // 4, place % 4 // 2, place % 2
            z = PAIR_Z[x % 2][group % 2][pair]
            home[group * count + place] = (group // 2 * 2 + core) * count + 4 * x + z
    return home


def vmem():
    return pl.BlockSpec(memory_space=pltpu.VMEM)


def smem():
    return pl.BlockSpec(memory_space=pltpu.SMEM)


PARAMS = pltpu.CompilerParams(vmem_limit_bytes=40 * 1024 * 1024)


def shape(*dims):
    return jax.ShapeDtypeStruct(dims, jnp.float32)


def shards(statistics, assignment):
    factors, slab, order = statistics.shape
    count = order // WIDTH
    devices = factors * count
    axes = ("fac", "jac")
    home = homes(factors, count)
    places = np.zeros(devices, np.int32)
    places[home] = np.arange(devices) % count
    me = lax.axis_index(axes).astype(jnp.int32).reshape(1)
    dealt = pl.pallas_call(
        deal_kernel,
        out_shape=shape(devices, slab, WIDTH),
        in_specs=[smem(), smem(), vmem()],
        out_specs=vmem(),
        compiler_params=PARAMS,
        name="deal",
    )(assignment, jnp.asarray(home), statistics)
    moved = lax.all_to_all(dealt, axes, split_axis=0, concat_axis=0, tiled=True)
    work = moved.reshape(order, WIDTH)
    places = jnp.asarray(places)
    store = pltpu.VMEM((WIDTH, WIDTH), jnp.float32)
    near, far = pl.pallas_call(
        first_kernel,
        out_shape=[shape(BLK, order + WIDTH)] * 2,
        in_specs=[smem(), smem(), vmem()],
        out_specs=[vmem()] * 2,
        scratch_shapes=[store],
        compiler_params=PARAMS,
        name="first_round",
    )(me, places, work)
    for later in range(1, ROUNDS + 1):
        goal = home if later < ROUNDS else np.arange(devices, dtype=np.int32)
        near_route, far_route = [], []
        for group in range(factors):
            for place in range(count):
                start = int(home[group * count + place])
                near_route.append((start, int(goal[group * count + (place ^ 1)])))
                far_route.append((start, int(goal[group * count + far_place(place, count)])))
        from_far = lax.ppermute(far, axes, far_route)
        from_near = lax.ppermute(near, axes, near_route)
        if later < ROUNDS:
            near, far = pl.pallas_call(
                functools.partial(next_kernel, order, later == ROUNDS - 1),
                out_shape=[shape(BLK, order + (later + 1) * WIDTH)] * 2,
                in_specs=[smem(), smem(), vmem(), vmem()],
                out_specs=[vmem()] * 2,
                scratch_shapes=[store],
                compiler_params=PARAMS,
                name="next_round",
            )(me, places, from_near, from_far)
    work, basis = pl.pallas_call(
        last_kernel,
        out_shape=[shape(order, WIDTH)] * 2,
        in_specs=[smem(), smem(), vmem(), vmem()],
        out_specs=[vmem()] * 2,
        compiler_params=PARAMS,
        name="output",
    )(me, jnp.asarray(support_table(count)), from_near, from_far)
    return work[None], basis[None]


def solution(mesh):
    return jax.shard_map(
        shards,
        mesh=mesh,
        in_specs=(P(None, ("fac", "jac"), None), P()),
        out_specs=(P("fac", None, "jac"), P("fac", None, "jac")),
        check_vma=False,
    )
```

```python
import functools

import jax
import jax.numpy as jnp
import numpy as np
from jax import lax
from jax.experimental import pallas as pl
from jax.experimental.pallas import tpu as pltpu
from jax.sharding import PartitionSpec as P

ROUNDS = 3
CHUNK = 512
CHAINS = (
    ((0, 1), (1, 1), (1, 0), (1, 3), (2, 3), (2, 0), (3, 0), (3, 3)),
    ((0, 0), (0, 3), (0, 2), (1, 2), (2, 2), (2, 1), (3, 1), (3, 2)),
)
BLK = 64
WIDTH = 2 * BLK
SECTIONS = 16
SUB = 8
GROUPS = BLK // SUB


def lane_ids(rows):
    return lax.broadcasted_iota(jnp.int32, (rows, WIDTH), 1)


def angles(alpha, beta, gamma):
    diff = beta - alpha
    square = diff * diff + 4.0 * gamma * gamma
    turns = square > 0
    inverse = jnp.where(turns, lax.rsqrt(jnp.where(turns, square, 1.0)), 0.0)
    along = diff * inverse
    lead = 1.0 + jnp.abs(along)
    cross = 2.0 * gamma * inverse * along
    scale = lax.rsqrt(lead * lead + cross * cross)
    return lead * scale, cross * scale


def small_rotation(gram, store, swapped):
    lanes = lane_ids(WIDTH)
    rows = lax.broadcasted_iota(jnp.int32, (WIDTH, WIDTH), 0)
    upper_half = lanes & BLK
    skew = ((rows - lanes) & (BLK - 1)) + upper_half
    store[...] = jnp.take_along_axis(gram, skew, axis=1).T
    low = lane_ids(SUB) < BLK
    aa, bb, tt, dd = [], [], [], []
    for b in range(GROUPS):
        top = store[pl.ds(b, SUB, stride=SUB), :]
        bot = store[pl.ds(BLK + b, SUB, stride=SUB), :]
        top_swap = pltpu.roll(top, BLK, 1)
        bot_swap = pltpu.roll(bot, BLK, 1)
        blocks = (
            jnp.where(low, top, top_swap),
            jnp.where(low, bot, bot_swap),
            jnp.where(low, top_swap, top),
            jnp.where(low, bot_swap, bot),
        )
        aa.append(jnp.where(swapped, blocks[3], blocks[0]))
        bb.append(jnp.where(swapped, blocks[2], blocks[1]))
        tt.append(jnp.where(swapped, blocks[1], blocks[2]))
        dd.append(jnp.where(swapped, blocks[0], blocks[3]))
    first_rows = lax.broadcasted_iota(jnp.int32, (SUB, WIDTH), 0)
    start = jnp.where(first_rows == 0, 1.0, 0.0).astype(jnp.float32)
    zero = jnp.zeros((SUB, WIDTH), jnp.float32)
    ru = [jnp.where(low, start, 0.0)] + [zero] * (GROUPS - 1)
    rl = [jnp.where(low, 0.0, start)] + [zero] * (GROUPS - 1)

    def spread(x, row):
        return jnp.broadcast_to(x[row:row + 1], (SUB, WIDTH))

    alpha, beta, gamma = spread(aa[0], 0), spread(dd[0], 0), spread(bb[0], 0)
    for section in range(SECTIONS):
        c, s = angles(alpha, beta, gamma)
        cc = [pltpu.roll(c, b, 1, stride=SUB, stride_axis=0) for b in range(GROUPS)]
        ss = [pltpu.roll(s, b, 1, stride=SUB, stride_axis=0) for b in range(GROUPS)]
        new_ru = [cc[b] * ru[b] - ss[b] * rl[b] for b in range(GROUPS)]
        new_rl = [ss[b] * ru[b] + cc[b] * rl[b] for b in range(GROUPS)]
        ru, rl = new_ru, new_rl
        if section == SECTIONS - 1:
            break
        rl = [pltpu.roll(rl[-1], 1, 0)] + rl[:-1]
        a1 = [cc[b] * aa[b] - ss[b] * bb[b] for b in range(GROUPS)]
        b1 = [ss[b] * aa[b] + cc[b] * bb[b] for b in range(GROUPS)]
        t1 = [cc[b] * tt[b] - ss[b] * dd[b] for b in range(GROUPS)]
        d1 = [ss[b] * tt[b] + cc[b] * dd[b] for b in range(GROUPS)]
        aa = [c * a1[b] - s * t1[b] for b in range(GROUPS)]
        t2 = [s * a1[b] + c * t1[b] for b in range(GROUPS)]
        b2 = [c * b1[b] - s * d1[b] for b in range(GROUPS)]
        d2 = [s * b1[b] + c * d1[b] for b in range(GROUPS)]
        new_alpha = c * (c * alpha - s * gamma) - s * (c * gamma - s * beta)
        new_beta = s * (s * alpha + c * gamma) + c * (s * gamma + c * beta)
        alpha, beta = new_alpha, pltpu.roll(new_beta, WIDTH - 1, 1)
        gamma = spread(b2[-1], SUB - 1)
        bb = [pltpu.roll(b2[-1], 1, 0)] + b2[:-1]
        t2 = t2[1:] + [pltpu.roll(t2[0], SUB - 1, 0)]
        tt = [pltpu.roll(x, WIDTH - 1, 1) for x in t2]
        dd = [pltpu.roll(x, WIDTH - 1, 1) for x in d2]
    for b in range(GROUPS):
        store[pl.ds(b, SUB, stride=SUB), :] = ru[b]
        store[pl.ds(BLK + b, SUB, stride=SUB), :] = rl[b]
    offset = jnp.where(upper_half == 0, 0, SECTIONS - 1)
    unskew = ((rows - lanes + offset) & (BLK - 1)) + upper_half
    return jnp.take_along_axis(store[...].T, unskew, axis=1)


def deal_kernel(assignment, stats, out, owners, slabs, sems):
    factors, _, order = stats.shape
    count = order // WIDTH
    copies = [pltpu.make_async_copy(stats.at[f], slabs.at[f], sems.at[f]) for f in range(factors)]
    for copy in copies:
        copy.start()
    table = pltpu.make_async_copy(assignment, owners, sems.at[factors])
    table.start()
    table.wait()
    for factor in range(factors):
        group = owners[factor]
        odd = group % 2 == 1
        base = group // 2 * (2 * count)
        copies[factor].wait()
        for place in range(count):
            home = base + jnp.where(odd, home_of(1, place, count), home_of(0, place, count))
            out[home] = slabs[factor, :, place * WIDTH:(place + 1) * WIDTH]


def pieces(x):
    high = x.astype(jnp.bfloat16)
    rest = x - high.astype(jnp.float32)
    middle = rest.astype(jnp.bfloat16)
    low = (rest - middle.astype(jnp.float32)).astype(jnp.bfloat16)
    return high, middle, low


def gram_of(parts):
    high, middle, low = parts
    left = jnp.concatenate([high, middle, low], axis=0)
    right = jnp.concatenate([high, middle], axis=0)
    full = lax.dot_general(left, right, (((1,), (1,)), ((), ())), preferred_element_type=jnp.float32)
    crossed = full[2 * WIDTH:, :WIDTH]
    small = full[WIDTH:2 * WIDTH, WIDTH:] + (crossed + crossed.T)
    return full[:WIDTH, :WIDTH] + (full[:WIDTH, WIDTH:] + full[WIDTH:2 * WIDTH, :WIDTH] + small)


def apply(rotation, parts, near, far, start, exact):
    high, middle, low = pieces(rotation)
    first = jnp.concatenate(
        [jnp.concatenate([high, middle], axis=1), jnp.concatenate([middle, high], axis=1)], axis=0
    )
    last = jnp.concatenate([low, high], axis=1)
    total = parts[0].shape[1]
    for begin in range(0, total, CHUNK):
        end = min(begin + CHUNK, total)
        part = [x[:, begin:end] for x in parts]
        both = jnp.dot(first, jnp.concatenate(part[:2], axis=0), preferred_element_type=jnp.float32)
        small = both[WIDTH:]
        if exact:
            small = small + jnp.dot(
                last, jnp.concatenate([part[0], part[2]], axis=0), preferred_element_type=jnp.float32
            )
        post(near, far, pl.ds(start + begin, end - begin), both[:WIDTH] + small)


def swap_halves(x, axis, swapped):
    return jnp.where(swapped, pltpu.roll(x, BLK, axis), x)


def leave_rotation(gram, store, place, swapped):
    rotation = small_rotation(gram, store, swapped).T
    bottom_first = jnp.logical_or(place == 0, place % 2 == 1)
    return swap_halves(rotation, 0, bottom_first)


def post(near, far, columns, block):
    near[:, columns] = block[:BLK]
    far[:, columns] = block[BLK:]


def first_kernel(me, places, work, far, near, store):
    place = places[me[0]]
    order = work.shape[0]
    parts = pieces(work[...].T)
    rotation = leave_rotation(gram_of(parts), store, place, False)
    apply(rotation, parts, near, far, 0, True)
    post(near, far, pl.ds(order, WIDTH), rotation)


def next_kernel(order, final, me, places, from_far, from_near, far, near, store):
    place = places[me[0]]
    swapped = place % 2 == 0
    parts = pieces(jnp.concatenate([from_near[:, :order], from_far[:, :order]], axis=0))
    rotation = leave_rotation(gram_of(parts), store, place, swapped)
    rotation = swap_halves(rotation, 1, swapped)
    apply(rotation, parts, near, far, 0, not final)
    blank = jnp.zeros((BLK, WIDTH), jnp.float32)
    near_basis = [from_near[:, c:c + WIDTH] for c in range(order, from_near.shape[1], WIDTH)]
    far_basis = [from_far[:, c:c + WIDTH] for c in range(order, from_far.shape[1], WIDTH)]
    if final:
        near_basis, far_basis = near_basis + [blank], [far_basis[1], blank, far_basis[0]]
    else:
        near_basis, far_basis = near_basis + [blank], [blank] + far_basis
    columns = [jnp.concatenate(halves, axis=0) for halves in zip(near_basis, far_basis)]
    apply(rotation, pieces(jnp.concatenate(columns, axis=1)), near, far, order, False)


def last_kernel(me, table, from_far, from_near, work, basis, work_store, basis_store, sems):
    order = work.shape[0]
    place = me[0] % table.shape[0]
    even = place % 2 == 0
    basis_store[...] = jnp.zeros_like(basis_store)
    chunks = (from_near.shape[1] - order) // WIDTH
    left_half = lane_ids(WIDTH) < BLK
    for chunk in range(chunks):
        columns = pl.ds(order + chunk * WIDTH, WIDTH)
        piece = jnp.concatenate([from_near[:, columns], from_far[:, columns]], axis=0).T
        piece = swap_halves(piece, 1, even)
        for half in range(2):
            row = pl.multiple_of(table[place, half * chunks + chunk] * WIDTH, WIDTH)
            left = jnp.logical_xor(even, half == 0)
            basis_store[pl.ds(row, WIDTH), :] += jnp.where(left_half == left, piece, 0.0)
    copies = [pltpu.make_async_copy(basis_store, basis, sems.at[0])]
    copies[0].start()
    for number, begin in enumerate(range(0, order, CHUNK)):
        rows = pl.ds(begin, CHUNK)
        near, far = from_near[:, rows], from_far[:, rows]
        pair = [jnp.where(even, far, near), jnp.where(even, near, far)]
        work_store[rows, :] = jnp.concatenate(pair, axis=0).T
        copies.append(pltpu.make_async_copy(work_store.at[rows], work.at[rows], sems.at[number + 1]))
        copies[-1].start()
    for copy in copies:
        copy.wait()


def far_place(place, count):
    return min(max(place + (1 if place % 2 else -1), 0), count - 1)


def support_table(count):
    far = [far_place(p, count) for p in range(count)]
    second = [[p ^ 1, far[p]] for p in range(count)]
    third = [[p, second[p ^ 1][1], second[far[p]][0]] for p in range(count)]
    return np.array([third[p ^ 1] + third[far[p]] for p in range(count)], np.int32)


def home_of(group, place, count):
    x, z = CHAINS[group % 2][place // 2]
    return (group // 2 * 2 + place % 2) * count + 4 * x + z


def vmem():
    return pl.BlockSpec(memory_space=pltpu.VMEM)


def smem():
    return pl.BlockSpec(memory_space=pltpu.SMEM)


def hbm():
    return pl.BlockSpec(memory_space=pltpu.HBM)


MIB = 1024 * 1024
PARAMS = pltpu.CompilerParams(vmem_limit_bytes=40 * MIB)
DEAL_PARAMS = pltpu.CompilerParams(vmem_limit_bytes=62 * MIB + MIB // 2)


def shape(*dims):
    return jax.ShapeDtypeStruct(dims, jnp.float32)


def shards(statistics, assignment):
    factors, slab, order = statistics.shape
    count = order // WIDTH
    devices = factors * count
    axes = ("fac", "jac")
    home = np.array([home_of(g, p, count) for g in range(factors) for p in range(count)], np.int32)
    places = np.zeros(devices, np.int32)
    places[home] = np.arange(devices) % count
    me = lax.axis_index(axes).astype(jnp.int32).reshape(1)
    dealt = pl.pallas_call(
        deal_kernel,
        out_shape=shape(devices, slab, WIDTH),
        in_specs=[hbm(), hbm()],
        out_specs=vmem(),
        scratch_shapes=[
            pltpu.SMEM((factors,), jnp.int32),
            pltpu.VMEM((factors, slab, order), jnp.float32),
            pltpu.SemaphoreType.DMA((factors + 1,)),
        ],
        compiler_params=DEAL_PARAMS,
        name="deal",
    )(assignment, statistics)
    moved = lax.all_to_all(dealt, axes, split_axis=0, concat_axis=0, tiled=True)
    work = moved.reshape(order, WIDTH)
    places = jnp.asarray(places)
    store = pltpu.VMEM((WIDTH, WIDTH), jnp.float32)
    far, near = pl.pallas_call(
        first_kernel,
        out_shape=[shape(BLK, order + WIDTH)] * 2,
        in_specs=[smem(), smem(), vmem()],
        out_specs=[vmem()] * 2,
        scratch_shapes=[store],
        compiler_params=PARAMS,
        name="first_round",
    )(me, places, work)
    for later in range(1, ROUNDS + 1):
        goal = home if later < ROUNDS else np.arange(devices, dtype=np.int32)
        near_route, far_route = [], []
        for group in range(factors):
            for place in range(count):
                start = int(home[group * count + place])
                near_route.append((start, int(goal[group * count + (place ^ 1)])))
                far_route.append((start, int(goal[group * count + far_place(place, count)])))
        from_far = lax.ppermute(far, axes, far_route)
        from_near = lax.ppermute(near, axes, near_route)
        if later < ROUNDS:
            far, near = pl.pallas_call(
                functools.partial(next_kernel, order, later == ROUNDS - 1),
                out_shape=[shape(BLK, order + (later + 1) * WIDTH)] * 2,
                in_specs=[smem(), smem(), vmem(), vmem()],
                out_specs=[vmem()] * 2,
                scratch_shapes=[store],
                compiler_params=PARAMS,
                name="next_round",
            )(me, places, from_far, from_near)
    work, basis = pl.pallas_call(
        last_kernel,
        out_shape=[shape(order, WIDTH)] * 2,
        in_specs=[smem(), smem(), vmem(), vmem()],
        out_specs=[hbm()] * 2,
        scratch_shapes=[pltpu.VMEM((order, WIDTH), jnp.float32)] * 2
        + [pltpu.SemaphoreType.DMA((1 + order // CHUNK,))],
        compiler_params=PARAMS,
        name="output",
    )(me, jnp.asarray(support_table(count)), from_far, from_near)
    return work[None], basis[None]


def solution(mesh):
    return jax.shard_map(
        shards,
        mesh=mesh,
        in_specs=(P(None, ("fac", "jac"), None), P()),
        out_specs=(P("fac", None, "jac"), P("fac", None, "jac")),
        check_vma=False,
    )
```

```python
import functools

import jax
import jax.numpy as jnp
import numpy as np
from jax import lax
from jax.experimental import pallas as pl
from jax.experimental.pallas import tpu as pltpu
from jax.sharding import PartitionSpec as P

ROUNDS = 3
CHUNK = 512
CHAINS = (
    ((0, 1), (0, 0), (1, 3), (1, 2), (2, 1), (2, 0), (3, 3), (3, 2)),
    ((0, 3), (0, 2), (1, 1), (1, 0), (2, 3), (2, 2), (3, 1), (3, 0)),
)
BLK = 64
WIDTH = 2 * BLK
SECTIONS = 16
SUB = 8
GROUPS = BLK // SUB


def lane_ids(rows):
    return lax.broadcasted_iota(jnp.int32, (rows, WIDTH), 1)


def angles(alpha, beta, gamma):
    diff = beta - alpha
    square = diff * diff + 4.0 * gamma * gamma
    turns = square > 0
    inverse = jnp.where(turns, lax.rsqrt(jnp.where(turns, square, 1.0)), 0.0)
    along = diff * inverse
    lead = 1.0 + jnp.abs(along)
    cross = 2.0 * gamma * inverse * along
    scale = lax.rsqrt(lead * lead + cross * cross)
    return lead * scale, cross * scale


def small_rotation(gram, store, swapped):
    lanes = lane_ids(WIDTH)
    rows = lax.broadcasted_iota(jnp.int32, (WIDTH, WIDTH), 0)
    upper_half = lanes & BLK
    skew = ((rows - lanes) & (BLK - 1)) + upper_half
    store[...] = jnp.take_along_axis(gram, skew, axis=1).T
    low = lane_ids(SUB) < BLK
    aa, bb, tt, dd = [], [], [], []
    for b in range(GROUPS):
        top = store[pl.ds(b, SUB, stride=SUB), :]
        bot = store[pl.ds(BLK + b, SUB, stride=SUB), :]
        top_swap = pltpu.roll(top, BLK, 1)
        bot_swap = pltpu.roll(bot, BLK, 1)
        blocks = (
            jnp.where(low, top, top_swap),
            jnp.where(low, bot, bot_swap),
            jnp.where(low, top_swap, top),
            jnp.where(low, bot_swap, bot),
        )
        aa.append(jnp.where(swapped, blocks[3], blocks[0]))
        bb.append(jnp.where(swapped, blocks[2], blocks[1]))
        tt.append(jnp.where(swapped, blocks[1], blocks[2]))
        dd.append(jnp.where(swapped, blocks[0], blocks[3]))
    first_rows = lax.broadcasted_iota(jnp.int32, (SUB, WIDTH), 0)
    start = jnp.where(first_rows == 0, 1.0, 0.0).astype(jnp.float32)
    zero = jnp.zeros((SUB, WIDTH), jnp.float32)
    ru = [jnp.where(low, start, 0.0)] + [zero] * (GROUPS - 1)
    rl = [jnp.where(low, 0.0, start)] + [zero] * (GROUPS - 1)

    def spread(x, row):
        return jnp.broadcast_to(x[row:row + 1], (SUB, WIDTH))

    alpha, beta, gamma = spread(aa[0], 0), spread(dd[0], 0), spread(bb[0], 0)
    for section in range(SECTIONS):
        c, s = angles(alpha, beta, gamma)
        cc = [pltpu.roll(c, b, 1, stride=SUB, stride_axis=0) for b in range(GROUPS)]
        ss = [pltpu.roll(s, b, 1, stride=SUB, stride_axis=0) for b in range(GROUPS)]
        new_ru = [cc[b] * ru[b] - ss[b] * rl[b] for b in range(GROUPS)]
        new_rl = [ss[b] * ru[b] + cc[b] * rl[b] for b in range(GROUPS)]
        ru, rl = new_ru, new_rl
        if section == SECTIONS - 1:
            break
        rl = [pltpu.roll(rl[-1], 1, 0)] + rl[:-1]
        a1 = [cc[b] * aa[b] - ss[b] * bb[b] for b in range(GROUPS)]
        b1 = [ss[b] * aa[b] + cc[b] * bb[b] for b in range(GROUPS)]
        t1 = [cc[b] * tt[b] - ss[b] * dd[b] for b in range(GROUPS)]
        d1 = [ss[b] * tt[b] + cc[b] * dd[b] for b in range(GROUPS)]
        aa = [c * a1[b] - s * t1[b] for b in range(GROUPS)]
        t2 = [s * a1[b] + c * t1[b] for b in range(GROUPS)]
        b2 = [c * b1[b] - s * d1[b] for b in range(GROUPS)]
        d2 = [s * b1[b] + c * d1[b] for b in range(GROUPS)]
        new_alpha = c * (c * alpha - s * gamma) - s * (c * gamma - s * beta)
        new_beta = s * (s * alpha + c * gamma) + c * (s * gamma + c * beta)
        alpha, beta = new_alpha, pltpu.roll(new_beta, WIDTH - 1, 1)
        gamma = spread(b2[-1], SUB - 1)
        bb = [pltpu.roll(b2[-1], 1, 0)] + b2[:-1]
        t2 = t2[1:] + [pltpu.roll(t2[0], SUB - 1, 0)]
        tt = [pltpu.roll(x, WIDTH - 1, 1) for x in t2]
        dd = [pltpu.roll(x, WIDTH - 1, 1) for x in d2]
    for b in range(GROUPS):
        store[pl.ds(b, SUB, stride=SUB), :] = ru[b]
        store[pl.ds(BLK + b, SUB, stride=SUB), :] = rl[b]
    offset = jnp.where(upper_half == 0, 0, SECTIONS - 1)
    unskew = ((rows - lanes + offset) & (BLK - 1)) + upper_half
    return jnp.take_along_axis(store[...].T, unskew, axis=1)


def deal_kernel(assignment, stats, out, owners, slabs, sems):
    factors, _, order = stats.shape
    count = order // WIDTH
    copies = [pltpu.make_async_copy(stats.at[f], slabs.at[f], sems.at[f]) for f in range(factors)]
    for copy in copies:
        copy.start()
    table = pltpu.make_async_copy(assignment, owners, sems.at[factors])
    table.start()
    table.wait()
    for factor in range(factors):
        group = owners[factor]
        odd = group % 2 == 1
        base = group // 2 * (2 * count)
        copies[factor].wait()
        for place in range(count):
            home = base + jnp.where(odd, home_of(1, place, count), home_of(0, place, count))
            out[home] = slabs[factor, :, place * WIDTH:(place + 1) * WIDTH]


def pieces(x):
    high = x.astype(jnp.bfloat16)
    rest = x - high.astype(jnp.float32)
    middle = rest.astype(jnp.bfloat16)
    low = (rest - middle.astype(jnp.float32)).astype(jnp.bfloat16)
    return high, middle, low


def gram_of(parts):
    high, middle, low = parts
    left = jnp.concatenate([high, middle, low], axis=0)
    right = jnp.concatenate([high, middle], axis=0)
    full = lax.dot_general(left, right, (((1,), (1,)), ((), ())), preferred_element_type=jnp.float32)
    crossed = full[2 * WIDTH:, :WIDTH]
    small = full[WIDTH:2 * WIDTH, WIDTH:] + (crossed + crossed.T)
    return full[:WIDTH, :WIDTH] + (full[:WIDTH, WIDTH:] + full[WIDTH:2 * WIDTH, :WIDTH] + small)


def apply(rotation, parts, near, far, start, exact):
    high, middle, low = pieces(rotation)
    first = jnp.concatenate(
        [jnp.concatenate([high, middle], axis=1), jnp.concatenate([middle, high], axis=1)], axis=0
    )
    last = jnp.concatenate([low, high], axis=1)
    total = parts[0].shape[1]
    for begin in range(0, total, CHUNK):
        end = min(begin + CHUNK, total)
        part = [x[:, begin:end] for x in parts]
        both = jnp.dot(first, jnp.concatenate(part[:2], axis=0), preferred_element_type=jnp.float32)
        small = both[WIDTH:]
        if exact:
            small = small + jnp.dot(
                last, jnp.concatenate([part[0], part[2]], axis=0), preferred_element_type=jnp.float32
            )
        post(near, far, pl.ds(start + begin, end - begin), both[:WIDTH] + small)


def swap_halves(x, axis, swapped):
    return jnp.where(swapped, pltpu.roll(x, BLK, axis), x)


def leave_rotation(gram, store, place, swapped):
    rotation = small_rotation(gram, store, swapped).T
    bottom_first = jnp.logical_or(place == 0, place % 2 == 1)
    return swap_halves(rotation, 0, bottom_first)


def post(near, far, columns, block):
    near[:, columns] = block[:BLK]
    far[:, columns] = block[BLK:]


def first_kernel(me, places, work, far, near, store):
    place = places[me[0]]
    order = work.shape[0]
    parts = pieces(work[...].T)
    rotation = leave_rotation(gram_of(parts), store, place, False)
    apply(rotation, parts, near, far, 0, True)
    post(near, far, pl.ds(order, WIDTH), rotation)


def next_kernel(order, final, me, places, from_far, from_near, far, near, store):
    place = places[me[0]]
    swapped = place % 2 == 0
    parts = pieces(jnp.concatenate([from_near[:, :order], from_far[:, :order]], axis=0))
    rotation = leave_rotation(gram_of(parts), store, place, swapped)
    rotation = swap_halves(rotation, 1, swapped)
    apply(rotation, parts, near, far, 0, not final)
    blank = jnp.zeros((BLK, WIDTH), jnp.float32)
    near_basis = [from_near[:, c:c + WIDTH] for c in range(order, from_near.shape[1], WIDTH)]
    far_basis = [from_far[:, c:c + WIDTH] for c in range(order, from_far.shape[1], WIDTH)]
    if final:
        near_basis, far_basis = near_basis + [blank], [far_basis[1], blank, far_basis[0]]
    else:
        near_basis, far_basis = near_basis + [blank], [blank] + far_basis
    columns = [jnp.concatenate(halves, axis=0) for halves in zip(near_basis, far_basis)]
    apply(rotation, pieces(jnp.concatenate(columns, axis=1)), near, far, order, False)


def last_kernel(me, table, from_far, from_near, work, basis, work_store, basis_store, sems):
    order = work.shape[0]
    place = me[0] % table.shape[0]
    even = place % 2 == 0
    basis_store[...] = jnp.zeros_like(basis_store)
    chunks = (from_near.shape[1] - order) // WIDTH
    left_half = lane_ids(WIDTH) < BLK
    for chunk in range(chunks):
        columns = pl.ds(order + chunk * WIDTH, WIDTH)
        piece = jnp.concatenate([from_near[:, columns], from_far[:, columns]], axis=0).T
        piece = swap_halves(piece, 1, even)
        for half in range(2):
            row = pl.multiple_of(table[place, half * chunks + chunk] * WIDTH, WIDTH)
            left = jnp.logical_xor(even, half == 0)
            basis_store[pl.ds(row, WIDTH), :] += jnp.where(left_half == left, piece, 0.0)
    copies = [pltpu.make_async_copy(basis_store, basis, sems.at[0])]
    copies[0].start()
    for number, begin in enumerate(range(0, order, CHUNK)):
        rows = pl.ds(begin, CHUNK)
        near, far = from_near[:, rows], from_far[:, rows]
        pair = [jnp.where(even, far, near), jnp.where(even, near, far)]
        work_store[rows, :] = jnp.concatenate(pair, axis=0).T
        copies.append(pltpu.make_async_copy(work_store.at[rows], work.at[rows], sems.at[number + 1]))
        copies[-1].start()
    for copy in copies:
        copy.wait()


def far_place(place, count):
    return min(max(place + (1 if place % 2 else -1), 0), count - 1)


def support_table(count):
    far = [far_place(p, count) for p in range(count)]
    second = [[p ^ 1, far[p]] for p in range(count)]
    third = [[p, second[p ^ 1][1], second[far[p]][0]] for p in range(count)]
    return np.array([third[p ^ 1] + third[far[p]] for p in range(count)], np.int32)


def home_of(group, place, count):
    x, z = CHAINS[group % 2][place // 2]
    return (group // 2 * 2 + place % 2) * count + 4 * x + z


def vmem():
    return pl.BlockSpec(memory_space=pltpu.VMEM)


def smem():
    return pl.BlockSpec(memory_space=pltpu.SMEM)


def hbm():
    return pl.BlockSpec(memory_space=pltpu.HBM)


MIB = 1024 * 1024
PARAMS = pltpu.CompilerParams(vmem_limit_bytes=40 * MIB)
DEAL_PARAMS = pltpu.CompilerParams(vmem_limit_bytes=62 * MIB + MIB // 2)


def shape(*dims):
    return jax.ShapeDtypeStruct(dims, jnp.float32)


def shards(statistics, assignment):
    factors, slab, order = statistics.shape
    count = order // WIDTH
    devices = factors * count
    axes = ("fac", "jac")
    home = np.array([home_of(g, p, count) for g in range(factors) for p in range(count)], np.int32)
    places = np.zeros(devices, np.int32)
    places[home] = np.arange(devices) % count
    me = lax.axis_index(axes).astype(jnp.int32).reshape(1)
    dealt = pl.pallas_call(
        deal_kernel,
        out_shape=shape(devices, slab, WIDTH),
        in_specs=[hbm(), hbm()],
        out_specs=vmem(),
        scratch_shapes=[
            pltpu.SMEM((factors,), jnp.int32),
            pltpu.VMEM((factors, slab, order), jnp.float32),
            pltpu.SemaphoreType.DMA((factors + 1,)),
        ],
        compiler_params=DEAL_PARAMS,
        name="deal",
    )(assignment, statistics)
    moved = lax.all_to_all(dealt, axes, split_axis=0, concat_axis=0, tiled=True)
    work = moved.reshape(order, WIDTH)
    places = jnp.asarray(places)
    store = pltpu.VMEM((WIDTH, WIDTH), jnp.float32)
    far, near = pl.pallas_call(
        first_kernel,
        out_shape=[shape(BLK, order + WIDTH)] * 2,
        in_specs=[smem(), smem(), vmem()],
        out_specs=[vmem()] * 2,
        scratch_shapes=[store],
        compiler_params=PARAMS,
        name="first_round",
    )(me, places, work)
    for later in range(1, ROUNDS + 1):
        goal = home if later < ROUNDS else np.arange(devices, dtype=np.int32)
        near_route, far_route = [], []
        for group in range(factors):
            for place in range(count):
                start = int(home[group * count + place])
                near_route.append((start, int(goal[group * count + (place ^ 1)])))
                far_route.append((start, int(goal[group * count + far_place(place, count)])))
        from_far = lax.ppermute(far, axes, far_route)
        from_near = lax.ppermute(near, axes, near_route)
        if later < ROUNDS:
            far, near = pl.pallas_call(
                functools.partial(next_kernel, order, later == ROUNDS - 1),
                out_shape=[shape(BLK, order + (later + 1) * WIDTH)] * 2,
                in_specs=[smem(), smem(), vmem(), vmem()],
                out_specs=[vmem()] * 2,
                scratch_shapes=[store],
                compiler_params=PARAMS,
                name="next_round",
            )(me, places, from_far, from_near)
    work, basis = pl.pallas_call(
        last_kernel,
        out_shape=[shape(order, WIDTH)] * 2,
        in_specs=[smem(), smem(), vmem(), vmem()],
        out_specs=[hbm()] * 2,
        scratch_shapes=[pltpu.VMEM((order, WIDTH), jnp.float32)] * 2
        + [pltpu.SemaphoreType.DMA((1 + order // CHUNK,))],
        compiler_params=PARAMS,
        name="output",
    )(me, jnp.asarray(support_table(count)), from_far, from_near)
    return work[None], basis[None]


def solution(mesh):
    return jax.shard_map(
        shards,
        mesh=mesh,
        in_specs=(P(None, ("fac", "jac"), None), P()),
        out_specs=(P("fac", None, "jac"), P("fac", None, "jac")),
        check_vma=False,
    )
```

```python
import functools

import jax
import jax.numpy as jnp
import numpy as np
from jax import lax
from jax.experimental import pallas as pl
from jax.experimental.pallas import tpu as pltpu
from jax.sharding import PartitionSpec as P

ROUNDS = 3
CHUNK = 512
CHAINS = (
    ((0, 1), (0, 0), (1, 3), (1, 2), (2, 1), (2, 0), (3, 3), (3, 2)),
    ((0, 3), (0, 2), (1, 1), (1, 0), (2, 3), (2, 2), (3, 1), (3, 0)),
)
BLK = 64
WIDTH = 2 * BLK
SECTIONS = 16
SUB = 8
GROUPS = BLK // SUB


def lane_ids(rows):
    return lax.broadcasted_iota(jnp.int32, (rows, WIDTH), 1)


def angles(alpha, beta, gamma):
    diff = beta - alpha
    square = diff * diff + 4.0 * gamma * gamma
    inverse = jnp.where(square > 0, lax.rsqrt(square), 0.0)
    along = diff * inverse
    lead = 1.0 + jnp.abs(along)
    cross = (2.0 * gamma) * inverse * along
    scale = lax.rsqrt(lead * lead + cross * cross)
    return lead * scale, cross * scale


def small_rotation(gram, store, swapped):
    lanes = lane_ids(WIDTH)
    rows = lax.broadcasted_iota(jnp.int32, (WIDTH, WIDTH), 0)
    upper_half = lanes & BLK
    skew = ((rows - lanes) & (BLK - 1)) + upper_half
    store[...] = jnp.take_along_axis(gram, skew, axis=1).T
    low = lane_ids(SUB) < BLK
    aa, bb, tt, dd = [], [], [], []
    for b in range(GROUPS):
        top = store[pl.ds(b, SUB, stride=SUB), :]
        bot = store[pl.ds(BLK + b, SUB, stride=SUB), :]
        top_swap = pltpu.roll(top, BLK, 1)
        bot_swap = pltpu.roll(bot, BLK, 1)
        blocks = (
            jnp.where(low, top, top_swap),
            jnp.where(low, bot, bot_swap),
            jnp.where(low, top_swap, top),
            jnp.where(low, bot_swap, bot),
        )
        aa.append(jnp.where(swapped, blocks[3], blocks[0]))
        bb.append(jnp.where(swapped, blocks[2], blocks[1]))
        tt.append(jnp.where(swapped, blocks[1], blocks[2]))
        dd.append(jnp.where(swapped, blocks[0], blocks[3]))
    first_rows = lax.broadcasted_iota(jnp.int32, (SUB, WIDTH), 0)
    start = jnp.where(first_rows == 0, 1.0, 0.0).astype(jnp.float32)
    zero = jnp.zeros((SUB, WIDTH), jnp.float32)
    ru = [jnp.where(low, start, 0.0)] + [zero] * (GROUPS - 1)
    rl = [jnp.where(low, 0.0, start)] + [zero] * (GROUPS - 1)

    def spread(x, row):
        return jnp.broadcast_to(x[row:row + 1], (SUB, WIDTH))

    alpha, beta, gamma = spread(aa[0], 0), spread(dd[0], 0), spread(bb[0], 0)
    for section in range(SECTIONS):
        ahead = [spread(x[-1], SUB - 1) for x in (aa, bb, tt, dd)]
        c, s = angles(alpha, beta, gamma)
        cc = [pltpu.roll(c, b, 1, stride=SUB, stride_axis=0) for b in range(GROUPS)]
        ss = [pltpu.roll(s, b, 1, stride=SUB, stride_axis=0) for b in range(GROUPS)]
        new_ru = [cc[b] * ru[b] - ss[b] * rl[b] for b in range(GROUPS)]
        new_rl = [ss[b] * ru[b] + cc[b] * rl[b] for b in range(GROUPS)]
        ru, rl = new_ru, new_rl
        if section == SECTIONS - 1:
            break
        rl = [pltpu.roll(rl[-1], 1, 0)] + rl[:-1]
        a1 = [cc[b] * aa[b] - ss[b] * bb[b] for b in range(GROUPS)]
        b1 = [ss[b] * aa[b] + cc[b] * bb[b] for b in range(GROUPS)]
        t1 = [cc[b] * tt[b] - ss[b] * dd[b] for b in range(GROUPS)]
        d1 = [ss[b] * tt[b] + cc[b] * dd[b] for b in range(GROUPS)]
        aa = [c * a1[b] - s * t1[b] for b in range(GROUPS)]
        t2 = [s * a1[b] + c * t1[b] for b in range(GROUPS)]
        b2 = [c * b1[b] - s * d1[b] for b in range(GROUPS)]
        d2 = [s * b1[b] + c * d1[b] for b in range(GROUPS)]
        new_alpha = c * (c * alpha - s * gamma) - s * (c * gamma - s * beta)
        new_beta = s * (s * alpha + c * gamma) + c * (s * gamma + c * beta)
        c_up, s_up = pltpu.roll(c, WIDTH - 1, 1), pltpu.roll(s, WIDTH - 1, 1)
        above = s_up * ahead[0] + c_up * ahead[1]
        below = s_up * ahead[2] + c_up * ahead[3]
        alpha, beta, gamma = new_alpha, pltpu.roll(new_beta, WIDTH - 1, 1), c * above - s * below
        bb = [pltpu.roll(b2[-1], 1, 0)] + b2[:-1]
        t2 = t2[1:] + [pltpu.roll(t2[0], SUB - 1, 0)]
        tt = [pltpu.roll(x, WIDTH - 1, 1) for x in t2]
        dd = [pltpu.roll(x, WIDTH - 1, 1) for x in d2]
    for b in range(GROUPS):
        store[pl.ds(b, SUB, stride=SUB), :] = ru[b]
        store[pl.ds(BLK + b, SUB, stride=SUB), :] = rl[b]
    offset = jnp.where(upper_half == 0, 0, SECTIONS - 1)
    unskew = ((rows - lanes + offset) & (BLK - 1)) + upper_half
    return jnp.take_along_axis(store[...].T, unskew, axis=1)


def deal_kernel(assignment, stats, out, owners, slabs, sems):
    factors, _, order = stats.shape
    count = order // WIDTH
    copies = [pltpu.make_async_copy(stats.at[f], slabs.at[f], sems.at[f]) for f in range(factors)]
    for copy in copies:
        copy.start()
    table = pltpu.make_async_copy(assignment, owners, sems.at[factors])
    table.start()
    table.wait()
    for factor in range(factors):
        group = owners[factor]
        odd = group % 2 == 1
        base = group // 2 * (2 * count)
        copies[factor].wait()
        for place in range(count):
            home = base + jnp.where(odd, home_of(1, place, count), home_of(0, place, count))
            out[home] = slabs[factor, :, place * WIDTH:(place + 1) * WIDTH]


def pieces(x):
    high = x.astype(jnp.bfloat16)
    rest = x - high.astype(jnp.float32)
    middle = rest.astype(jnp.bfloat16)
    low = (rest - middle.astype(jnp.float32)).astype(jnp.bfloat16)
    return high, middle, low


def gram_of(parts):
    high, middle, low = parts
    left = jnp.concatenate([high, middle, low], axis=0)
    right = jnp.concatenate([high, middle], axis=0)
    full = lax.dot_general(left, right, (((1,), (1,)), ((), ())), preferred_element_type=jnp.float32)
    crossed = full[2 * WIDTH:, :WIDTH]
    small = full[WIDTH:2 * WIDTH, WIDTH:] + (crossed + crossed.T)
    return full[:WIDTH, :WIDTH] + (full[:WIDTH, WIDTH:] + full[WIDTH:2 * WIDTH, :WIDTH] + small)


def apply(rotation, parts, near, far, start, exact):
    high, middle, low = pieces(rotation)
    first = jnp.concatenate(
        [jnp.concatenate([high, middle], axis=1), jnp.concatenate([middle, high], axis=1)], axis=0
    )
    last = jnp.concatenate([low, high], axis=1)
    total = parts[0].shape[1]
    for begin in range(0, total, CHUNK):
        end = min(begin + CHUNK, total)
        part = [x[:, begin:end] for x in parts]
        both = jnp.dot(first, jnp.concatenate(part[:2], axis=0), preferred_element_type=jnp.float32)
        small = both[WIDTH:]
        if exact:
            small = small + jnp.dot(
                last, jnp.concatenate([part[0], part[2]], axis=0), preferred_element_type=jnp.float32
            )
        post(near, far, pl.ds(start + begin, end - begin), both[:WIDTH] + small)


def swap_halves(x, axis, swapped):
    return jnp.where(swapped, pltpu.roll(x, BLK, axis), x)


def place_here():
    cell = lax.axis_index("jac")
    pair = 0
    for chain in CHAINS:
        for number, (x, z) in enumerate(chain):
            pair = jnp.where(cell == 4 * x + z, number, pair)
    return 2 * pair + lax.axis_index("fac") % 2


def leave_rotation(gram, store, place, swapped):
    rotation = small_rotation(gram, store, swapped).T
    bottom_first = jnp.logical_or(place == 0, place % 2 == 1)
    return swap_halves(rotation, 0, bottom_first)


def post(near, far, columns, block):
    near[:, columns] = block[:BLK]
    far[:, columns] = block[BLK:]


def first_kernel(work, far, near, store):
    place = place_here()
    order = work.shape[0]
    parts = pieces(work[...].T)
    rotation = leave_rotation(gram_of(parts), store, place, False)
    apply(rotation, parts, near, far, 0, True)
    post(near, far, pl.ds(order, WIDTH), rotation)


def next_kernel(order, final, from_far, from_near, far, near, store):
    place = place_here()
    swapped = place % 2 == 0
    parts = pieces(jnp.concatenate([from_near[:, :order], from_far[:, :order]], axis=0))
    rotation = leave_rotation(gram_of(parts), store, place, swapped)
    rotation = swap_halves(rotation, 1, swapped)
    apply(rotation, parts, near, far, 0, not final)
    blank = jnp.zeros((BLK, WIDTH), jnp.float32)
    near_basis = [from_near[:, c:c + WIDTH] for c in range(order, from_near.shape[1], WIDTH)]
    far_basis = [from_far[:, c:c + WIDTH] for c in range(order, from_far.shape[1], WIDTH)]
    if final:
        near_basis, far_basis = near_basis + [blank], [far_basis[1], blank, far_basis[0]]
    else:
        near_basis, far_basis = near_basis + [blank], [blank] + far_basis
    columns = [jnp.concatenate(halves, axis=0) for halves in zip(near_basis, far_basis)]
    apply(rotation, pieces(jnp.concatenate(columns, axis=1)), near, far, order, False)


def last_kernel(from_far, from_near, work, basis, work_store, basis_store, sems):
    order = work.shape[0]
    place = lax.axis_index("jac")
    count = lax.axis_size("jac")
    next_chip = far_place(place, count)
    rows = [
        [place ^ 1, next_chip, far_place(place ^ 1, count) ^ 1],
        [next_chip, far_place(next_chip ^ 1, count), far_place(next_chip, count) ^ 1],
    ]
    even = place % 2 == 0
    basis_store[...] = jnp.zeros_like(basis_store)
    chunks = (from_near.shape[1] - order) // WIDTH
    left_half = lane_ids(WIDTH) < BLK
    for chunk in range(chunks):
        columns = pl.ds(order + chunk * WIDTH, WIDTH)
        piece = jnp.concatenate([from_near[:, columns], from_far[:, columns]], axis=0).T
        piece = swap_halves(piece, 1, even)
        for half in range(2):
            row = pl.multiple_of(rows[half][chunk] * WIDTH, WIDTH)
            left = jnp.logical_xor(even, half == 0)
            basis_store[pl.ds(row, WIDTH), :] += jnp.where(left_half == left, piece, 0.0)
    copies = [pltpu.make_async_copy(basis_store, basis, sems.at[0])]
    copies[0].start()
    for number, begin in enumerate(range(0, order, CHUNK)):
        rows = pl.ds(begin, CHUNK)
        near, far = from_near[:, rows], from_far[:, rows]
        pair = [jnp.where(even, far, near), jnp.where(even, near, far)]
        work_store[rows, :] = jnp.concatenate(pair, axis=0).T
        copies.append(pltpu.make_async_copy(work_store.at[rows], work.at[rows], sems.at[number + 1]))
        copies[-1].start()
    for copy in copies:
        copy.wait()


def far_place(place, count):
    return jnp.clip(place + 2 * (place % 2) - 1, 0, count - 1)


def home_of(group, place, count):
    x, z = CHAINS[group % 2][place // 2]
    return (group // 2 * 2 + place % 2) * count + 4 * x + z


def vmem():
    return pl.BlockSpec(memory_space=pltpu.VMEM)


def hbm():
    return pl.BlockSpec(memory_space=pltpu.HBM)


MIB = 1024 * 1024
PARAMS = pltpu.CompilerParams(vmem_limit_bytes=40 * MIB)
DEAL_PARAMS = pltpu.CompilerParams(vmem_limit_bytes=62 * MIB + MIB // 2)


def shape(*dims):
    return jax.ShapeDtypeStruct(dims, jnp.float32)


def shards(statistics, assignment):
    factors, slab, order = statistics.shape
    count = order // WIDTH
    devices = factors * count
    axes = ("fac", "jac")
    home = np.array([home_of(g, p, count) for g in range(factors) for p in range(count)], np.int32)
    dealt = pl.pallas_call(
        deal_kernel,
        out_shape=shape(devices, slab, WIDTH),
        in_specs=[hbm(), hbm()],
        out_specs=vmem(),
        scratch_shapes=[
            pltpu.SMEM((factors,), jnp.int32),
            pltpu.VMEM((factors, slab, order), jnp.float32),
            pltpu.SemaphoreType.DMA((factors + 1,)),
        ],
        compiler_params=DEAL_PARAMS,
        name="deal",
    )(assignment, statistics)
    moved = lax.all_to_all(dealt, axes, split_axis=0, concat_axis=0, tiled=True)
    work = moved.reshape(order, WIDTH)
    store = pltpu.VMEM((WIDTH, WIDTH), jnp.float32)
    far, near = pl.pallas_call(
        first_kernel,
        out_shape=[shape(BLK, order + WIDTH)] * 2,
        in_specs=[vmem()],
        out_specs=[vmem()] * 2,
        scratch_shapes=[store],
        compiler_params=PARAMS,
        name="first_round",
    )(work)
    for later in range(1, ROUNDS + 1):
        goal = home if later < ROUNDS else np.arange(devices, dtype=np.int32)
        near_route, far_route = [], []
        for group in range(factors):
            for place in range(count):
                start = int(home[group * count + place])
                near_route.append((start, int(goal[group * count + (place ^ 1)])))
                other = min(max(place + 2 * (place % 2) - 1, 0), count - 1)
                far_route.append((start, int(goal[group * count + other])))
        from_far = lax.ppermute(far, axes, far_route)
        from_near = lax.ppermute(near, axes, near_route)
        if later < ROUNDS:
            far, near = pl.pallas_call(
                functools.partial(next_kernel, order, later == ROUNDS - 1),
                out_shape=[shape(BLK, order + (later + 1) * WIDTH)] * 2,
                in_specs=[vmem(), vmem()],
                out_specs=[vmem()] * 2,
                scratch_shapes=[store],
                compiler_params=PARAMS,
                name="next_round",
            )(from_far, from_near)
    work, basis = pl.pallas_call(
        last_kernel,
        out_shape=[shape(order, WIDTH)] * 2,
        in_specs=[vmem(), vmem()],
        out_specs=[hbm()] * 2,
        scratch_shapes=[pltpu.VMEM((order, WIDTH), jnp.float32)] * 2
        + [pltpu.SemaphoreType.DMA((1 + order // CHUNK,))],
        compiler_params=PARAMS,
        name="output",
    )(from_far, from_near)
    return work[None], basis[None]


def solution(mesh):
    return jax.shard_map(
        shards,
        mesh=mesh,
        in_specs=(P(None, ("fac", "jac"), None), P()),
        out_specs=(P("fac", None, "jac"), P("fac", None, "jac")),
        check_vma=False,
    )
```

```python
import functools

import jax
import jax.numpy as jnp
import numpy as np
from jax import lax
from jax.experimental import pallas as pl
from jax.experimental.pallas import tpu as pltpu
from jax.sharding import PartitionSpec as P

ROUNDS = 3
CHUNK = 512
CHAINS = (
    ((0, 1), (0, 0), (1, 3), (1, 2), (2, 1), (2, 0), (3, 3), (3, 2)),
    ((0, 3), (0, 2), (1, 1), (1, 0), (2, 3), (2, 2), (3, 1), (3, 0)),
)
BLK = 64
WIDTH = 2 * BLK
SECTIONS = 16
SUB = 8
GROUPS = SECTIONS // SUB


def lane_ids(rows):
    return lax.broadcasted_iota(jnp.int32, (rows, WIDTH), 1)


def angles(alpha, beta, gamma):
    diff = beta - alpha
    square = diff * diff + 4.0 * gamma * gamma
    inverse = jnp.where(square > 0, lax.rsqrt(square), 0.0)
    along = diff * inverse
    lead = 1.0 + jnp.abs(along)
    cross = (2.0 * gamma) * inverse * along
    scale = lax.rsqrt(lead * lead + cross * cross)
    return lead * scale, cross * scale


def small_rotation(gram, store, swapped):
    lanes = lane_ids(WIDTH)
    rows = lax.broadcasted_iota(jnp.int32, (WIDTH, WIDTH), 0)
    reach = SECTIONS - 1 - (lanes & (SECTIONS - 1))
    skew = ((rows + reach) & (BLK - 1)) + jnp.where((lanes & SECTIONS) == 0, 0, BLK)
    store[...] = jnp.take_along_axis(gram, skew, axis=1).T
    low = lane_ids(SUB) < BLK
    sublane = lax.broadcasted_iota(jnp.int32, (SUB, WIDTH), 0)
    aa, bb, tt, dd = [], [], [], []
    for v in range(GROUPS):
        begin = SECTIONS - SUB * (v + 1)
        top, bot = store[begin:begin + SUB, :], store[SECTIONS + begin:SECTIONS + begin + SUB, :]
        top_swap, bot_swap = pltpu.roll(top, BLK, 1), pltpu.roll(bot, BLK, 1)
        blocks = (
            jnp.where(low, top, top_swap),
            jnp.where(low, bot, bot_swap),
            jnp.where(low, top_swap, top),
            jnp.where(low, bot_swap, bot),
        )
        aa.append(jnp.where(swapped, blocks[3], blocks[0]))
        bb.append(jnp.where(swapped, blocks[2], blocks[1]))
        tt.append(jnp.where(swapped, blocks[1], blocks[2]))
        dd.append(jnp.where(swapped, blocks[0], blocks[3]))
    start = jnp.where(sublane == 0, 1.0, 0.0).astype(jnp.float32)
    zero = jnp.zeros((SUB, WIDTH), jnp.float32)
    ru = [jnp.where(low, start, 0.0)] + [zero] * (GROUPS - 1)
    rl = [jnp.where(low, 0.0, start)] + [zero] * (GROUPS - 1)

    def spread(x, row):
        return jnp.broadcast_to(x[row:row + 1], (SUB, WIDTH))

    alpha, beta, gamma = (spread(x[0], SUB - 1) for x in (aa, dd, bb))
    a_next, b_next, t_next, d_next = (spread(x[0], SUB - 2) for x in (aa, bb, tt, dd))
    for section in range(SECTIONS):
        c, s = angles(alpha, beta, gamma)
        c_up, s_up = pltpu.roll(c, WIDTH - 1, 1), pltpu.roll(s, WIDTH - 1, 1)
        for v in range(section // SUB + 1):
            cc = pltpu.roll(c, SUB * v, 1, stride=1, stride_axis=0)
            ss = pltpu.roll(s, SUB * v, 1, stride=1, stride_axis=0)
            ru[v], rl[v] = cc * ru[v] - ss * rl[v], ss * ru[v] + cc * rl[v]
        if section == SECTIONS - 1:
            break
        moved = [pltpu.roll(x, 1, 0) for x in rl]
        rl = [jnp.where(sublane == 0, before, x) for before, x in zip([zero] + moved[:-1], moved)]
        a1, t1 = c * alpha - s * gamma, c * gamma - s * beta
        new_beta = s * (s * alpha + c * gamma) + c * (s * gamma + c * beta)
        alpha, beta, rest = c * a1 - s * t1, pltpu.roll(new_beta, WIDTH - 1, 1), s * a1 + c * t1
        b1, d1 = s_up * a_next + c_up * b_next, s_up * t_next + c_up * d_next
        gamma = c * b1 - s * d1
        if section == SECTIONS - 2:
            continue
        a1, t1 = c_up * a_next - s_up * b_next, c_up * t_next - s_up * d_next
        a_next = c * a1 - s * t1
        t_next, d_next = pltpu.roll(rest, WIDTH - 1, 1), pltpu.roll(s * b1 + c * d1, WIDTH - 1, 1)
        kept = (SECTIONS - 1 - section) // SUB + 1
        aa, bb, tt, dd = aa[:kept], bb[:kept], tt[:kept], dd[:kept]
        for v in range(kept):
            cc = pltpu.roll(c, BLK - SUB * (v + 1) + 1, 1, stride=1, stride_axis=0)
            ss = pltpu.roll(s, BLK - SUB * (v + 1) + 1, 1, stride=1, stride_axis=0)
            a1, b1 = cc * aa[v] - ss * bb[v], ss * aa[v] + cc * bb[v]
            t1, d1 = cc * tt[v] - ss * dd[v], ss * tt[v] + cc * dd[v]
            b2 = c * b1 - s * d1
            if v == 0:
                b_next = spread(b2, SUB - 3)
            aa[v], bb[v] = c * a1 - s * t1, pltpu.roll(b2, 1, 0)
            tt[v] = pltpu.roll(pltpu.roll(s * a1 + c * t1, WIDTH - 1, 1), SUB - 1, 0)
            dd[v] = pltpu.roll(s * b1 + c * d1, WIDTH - 1, 1)
        bb = [jnp.where(sublane == 0, after, x) for x, after in zip(bb, bb[1:] + [zero])]
        tt = [jnp.where(sublane == SUB - 1, before, x) for before, x in zip([gamma] + tt[:-1], tt)]
    for v in range(GROUPS):
        store[SUB * v:SUB * (v + 1), :] = ru[v]
        store[SECTIONS + SUB * v:SECTIONS + SUB * (v + 1), :] = rl[v]
    upper = (lanes & BLK) == 0
    diagonal = (rows - lanes + jnp.where(upper, 0, SECTIONS - 1)) & (BLK - 1)
    index = (diagonal & (SECTIONS - 1)) + jnp.where(upper, 0, SECTIONS)
    return jnp.where(diagonal < SECTIONS, jnp.take_along_axis(store[...].T, index, axis=1), 0.0)


def deal_kernel(assignment, stats, out, owners, slabs, sems):
    factors, _, order = stats.shape
    count = order // WIDTH
    copies = [pltpu.make_async_copy(stats.at[f], slabs.at[f], sems.at[f]) for f in range(factors)]
    for copy in copies:
        copy.start()
    table = pltpu.make_async_copy(assignment, owners, sems.at[factors])
    table.start()
    table.wait()
    for factor in range(factors):
        group = owners[factor]
        odd = group % 2 == 1
        base = group // 2 * (2 * count)
        copies[factor].wait()
        for place in range(count):
            home = base + jnp.where(odd, home_of(1, place, count), home_of(0, place, count))
            out[home] = slabs[factor, :, place * WIDTH:(place + 1) * WIDTH]


def pieces(x):
    high = x.astype(jnp.bfloat16)
    rest = x - high.astype(jnp.float32)
    middle = rest.astype(jnp.bfloat16)
    low = (rest - middle.astype(jnp.float32)).astype(jnp.bfloat16)
    return high, middle, low


def gram_of(parts, across):
    full = jnp.dot(jnp.concatenate(parts, axis=0), across, preferred_element_type=jnp.float32)
    crossed = full[2 * WIDTH:, :WIDTH]
    small = full[WIDTH:2 * WIDTH, WIDTH:] + (crossed + crossed.T)
    return full[:WIDTH, :WIDTH] + (full[:WIDTH, WIDTH:] + full[WIDTH:2 * WIDTH, :WIDTH] + small)


def apply(rotation, parts, near, far, start, exact):
    high, middle, low = pieces(rotation)
    first = jnp.concatenate(
        [jnp.concatenate([high, middle], axis=1), jnp.concatenate([middle, high], axis=1)], axis=0
    )
    last = jnp.concatenate([low, high], axis=1)
    total = parts[0].shape[1]
    for begin in range(0, total, CHUNK):
        end = min(begin + CHUNK, total)
        part = [x[:, begin:end] for x in parts]
        both = jnp.dot(first, jnp.concatenate(part[:2], axis=0), preferred_element_type=jnp.float32)
        small = both[WIDTH:]
        if exact:
            small = small + jnp.dot(
                last, jnp.concatenate([part[0], part[2]], axis=0), preferred_element_type=jnp.float32
            )
        post(near, far, pl.ds(start + begin, end - begin), both[:WIDTH] + small)


def swap_halves(x, axis, swapped):
    return jnp.where(swapped, pltpu.roll(x, BLK, axis), x)


def place_here():
    cell = lax.axis_index("jac")
    pair = 0
    for chain in CHAINS:
        for number, (x, z) in enumerate(chain):
            pair = jnp.where(cell == 4 * x + z, number, pair)
    return 2 * pair + lax.axis_index("fac") % 2


def leave_rotation(gram, store, place, swapped):
    rotation = small_rotation(gram, store, swapped).T
    bottom_first = jnp.logical_or(place == 0, place % 2 == 1)
    return swap_halves(rotation, 0, bottom_first)


def post(near, far, columns, block):
    near[:, columns] = block[:BLK]
    far[:, columns] = block[BLK:]


def first_kernel(work, far, near, store):
    place = place_here()
    order = work.shape[0]
    straight = work[...]
    parts = pieces(straight.T)
    across = jnp.concatenate(pieces(straight)[:2], axis=1)
    rotation = leave_rotation(gram_of(parts, across), store, place, False)
    apply(rotation, parts, near, far, 0, True)
    post(near, far, pl.ds(order, WIDTH), rotation)


def next_kernel(order, final, from_far, from_near, far, near, store):
    place = place_here()
    swapped = place % 2 == 0
    parts = pieces(jnp.concatenate([from_near[:, :order], from_far[:, :order]], axis=0))
    across = jnp.concatenate(parts[:2], axis=0).T
    rotation = leave_rotation(gram_of(parts, across), store, place, swapped)
    rotation = swap_halves(rotation, 1, swapped)
    apply(rotation, parts, near, far, 0, not final)
    blank = jnp.zeros((BLK, WIDTH), jnp.float32)
    near_basis = [from_near[:, c:c + WIDTH] for c in range(order, from_near.shape[1], WIDTH)]
    far_basis = [from_far[:, c:c + WIDTH] for c in range(order, from_far.shape[1], WIDTH)]
    if final:
        near_basis, far_basis = near_basis + [blank], [far_basis[1], blank, far_basis[0]]
    else:
        near_basis, far_basis = near_basis + [blank], [blank] + far_basis
    columns = [jnp.concatenate(halves, axis=0) for halves in zip(near_basis, far_basis)]
    apply(rotation, pieces(jnp.concatenate(columns, axis=1)), near, far, order, False)


def last_kernel(from_far, from_near, work, basis, work_store, basis_store, sems):
    order = work.shape[0]
    place = lax.axis_index("jac")
    count = lax.axis_size("jac")
    next_chip = far_place(place, count)
    rows = [
        [place ^ 1, next_chip, far_place(place ^ 1, count) ^ 1],
        [next_chip, far_place(next_chip ^ 1, count), far_place(next_chip, count) ^ 1],
    ]
    even = place % 2 == 0
    basis_store[...] = jnp.zeros_like(basis_store)
    chunks = (from_near.shape[1] - order) // WIDTH
    left_half = lane_ids(WIDTH) < BLK
    for chunk in range(chunks):
        columns = pl.ds(order + chunk * WIDTH, WIDTH)
        piece = jnp.concatenate([from_near[:, columns], from_far[:, columns]], axis=0).T
        piece = swap_halves(piece, 1, even)
        for half in range(2):
            row = pl.multiple_of(rows[half][chunk] * WIDTH, WIDTH)
            left = jnp.logical_xor(even, half == 0)
            basis_store[pl.ds(row, WIDTH), :] += jnp.where(left_half == left, piece, 0.0)
    copies = [pltpu.make_async_copy(basis_store, basis, sems.at[0])]
    copies[0].start()
    for number, begin in enumerate(range(0, order, CHUNK)):
        rows = pl.ds(begin, CHUNK)
        near, far = from_near[:, rows], from_far[:, rows]
        pair = [jnp.where(even, far, near), jnp.where(even, near, far)]
        work_store[rows, :] = jnp.concatenate(pair, axis=0).T
        copies.append(pltpu.make_async_copy(work_store.at[rows], work.at[rows], sems.at[number + 1]))
        copies[-1].start()
    for copy in copies:
        copy.wait()


def far_place(place, count):
    return jnp.clip(place + 2 * (place % 2) - 1, 0, count - 1)


def home_of(group, place, count):
    x, z = CHAINS[group % 2][place // 2]
    return (group // 2 * 2 + place % 2) * count + 4 * x + z


def vmem():
    return pl.BlockSpec(memory_space=pltpu.VMEM)


def hbm():
    return pl.BlockSpec(memory_space=pltpu.HBM)


MIB = 1024 * 1024
PARAMS = pltpu.CompilerParams(vmem_limit_bytes=40 * MIB)
DEAL_PARAMS = pltpu.CompilerParams(vmem_limit_bytes=62 * MIB + MIB // 2)


def shape(*dims):
    return jax.ShapeDtypeStruct(dims, jnp.float32)


def shards(statistics, assignment):
    factors, slab, order = statistics.shape
    count = order // WIDTH
    devices = factors * count
    axes = ("fac", "jac")
    home = np.array([home_of(g, p, count) for g in range(factors) for p in range(count)], np.int32)
    dealt = pl.pallas_call(
        deal_kernel,
        out_shape=shape(devices, slab, WIDTH),
        in_specs=[hbm(), hbm()],
        out_specs=vmem(),
        scratch_shapes=[
            pltpu.SMEM((factors,), jnp.int32),
            pltpu.VMEM((factors, slab, order), jnp.float32),
            pltpu.SemaphoreType.DMA((factors + 1,)),
        ],
        compiler_params=DEAL_PARAMS,
        name="deal",
    )(assignment, statistics)
    moved = lax.all_to_all(dealt, axes, split_axis=0, concat_axis=0, tiled=True)
    work = moved.reshape(order, WIDTH)
    store = pltpu.VMEM((WIDTH, WIDTH), jnp.float32)
    far, near = pl.pallas_call(
        first_kernel,
        out_shape=[shape(BLK, order + WIDTH)] * 2,
        in_specs=[vmem()],
        out_specs=[vmem()] * 2,
        scratch_shapes=[store],
        compiler_params=PARAMS,
        name="first_round",
    )(work)
    for later in range(1, ROUNDS + 1):
        goal = home if later < ROUNDS else np.arange(devices, dtype=np.int32)
        near_route, far_route = [], []
        for group in range(factors):
            for place in range(count):
                start = int(home[group * count + place])
                near_route.append((start, int(goal[group * count + (place ^ 1)])))
                other = min(max(place + 2 * (place % 2) - 1, 0), count - 1)
                far_route.append((start, int(goal[group * count + other])))
        from_far = lax.ppermute(far, axes, far_route)
        from_near = lax.ppermute(near, axes, near_route)
        if later < ROUNDS:
            far, near = pl.pallas_call(
                functools.partial(next_kernel, order, later == ROUNDS - 1),
                out_shape=[shape(BLK, order + (later + 1) * WIDTH)] * 2,
                in_specs=[vmem(), vmem()],
                out_specs=[vmem()] * 2,
                scratch_shapes=[store],
                compiler_params=PARAMS,
                name="next_round",
            )(from_far, from_near)
    work, basis = pl.pallas_call(
        last_kernel,
        out_shape=[shape(order, WIDTH)] * 2,
        in_specs=[vmem(), vmem()],
        out_specs=[hbm()] * 2,
        scratch_shapes=[pltpu.VMEM((order, WIDTH), jnp.float32)] * 2
        + [pltpu.SemaphoreType.DMA((1 + order // CHUNK,))],
        compiler_params=PARAMS,
        name="output",
    )(from_far, from_near)
    return work[None], basis[None]


def solution(mesh):
    return jax.shard_map(
        shards,
        mesh=mesh,
        in_specs=(P(None, ("fac", "jac"), None), P()),
        out_specs=(P("fac", None, "jac"), P("fac", None, "jac")),
        check_vma=False,
    )
```

```python
import functools

import jax
import jax.numpy as jnp
import numpy as np
from jax import lax
from jax.experimental import pallas as pl
from jax.experimental.pallas import tpu as pltpu
from jax.sharding import PartitionSpec as P

ROUNDS = 3
CHUNK = 512
CHAINS = (
    ((0, 1), (0, 0), (1, 3), (1, 2), (2, 1), (2, 0), (3, 3), (3, 2)),
    ((0, 3), (0, 2), (1, 1), (1, 0), (2, 3), (2, 2), (3, 1), (3, 0)),
)
BLK = 64
WIDTH = 2 * BLK
SECTIONS = 16
SUB = 8
GROUPS = SECTIONS // SUB


def lane_ids(rows):
    return lax.broadcasted_iota(jnp.int32, (rows, WIDTH), 1)


def angles(alpha, beta, gamma):
    diff = beta - alpha
    square = diff * diff + 4.0 * gamma * gamma
    inverse = jnp.where(square > 0, lax.rsqrt(square), 0.0)
    along = diff * inverse
    lead = 1.0 + jnp.abs(along)
    cross = (2.0 * gamma) * inverse * along
    scale = lax.rsqrt(lead * lead + cross * cross)
    return lead * scale, cross * scale


def small_rotation(gram, store, swapped):
    lanes = lane_ids(WIDTH)
    rows = lax.broadcasted_iota(jnp.int32, (WIDTH, WIDTH), 0)
    reach = SECTIONS - 1 - (lanes & (SECTIONS - 1))
    skew = ((rows + reach) & (BLK - 1)) + jnp.where((lanes & SECTIONS) == 0, 0, BLK)
    store[...] = jnp.take_along_axis(gram, skew, axis=1).T
    low = lane_ids(SUB) < BLK
    sublane = lax.broadcasted_iota(jnp.int32, (SUB, WIDTH), 0)
    aa, bb, tt, dd = [], [], [], []
    for v in range(GROUPS):
        begin = SECTIONS - SUB * (v + 1)
        top, bot = store[begin:begin + SUB, :], store[SECTIONS + begin:SECTIONS + begin + SUB, :]
        top_swap, bot_swap = pltpu.roll(top, BLK, 1), pltpu.roll(bot, BLK, 1)
        blocks = (
            jnp.where(low, top, top_swap),
            jnp.where(low, bot, bot_swap),
            jnp.where(low, top_swap, top),
            jnp.where(low, bot_swap, bot),
        )
        aa.append(jnp.where(swapped, blocks[3], blocks[0]))
        bb.append(jnp.where(swapped, blocks[2], blocks[1]))
        tt.append(jnp.where(swapped, blocks[1], blocks[2]))
        dd.append(jnp.where(swapped, blocks[0], blocks[3]))
    start = jnp.where(sublane == 0, 1.0, 0.0).astype(jnp.float32)
    zero = jnp.zeros((SUB, WIDTH), jnp.float32)
    ru = [jnp.where(low, start, 0.0)] + [zero] * (GROUPS - 1)
    rl = [jnp.where(low, 0.0, start)] + [zero] * (GROUPS - 1)

    def spread(x, row):
        return jnp.broadcast_to(x[row:row + 1], (SUB, WIDTH))

    alpha, beta, gamma = (spread(x[0], SUB - 1) for x in (aa, dd, bb))
    a_next, b_next, t_next, d_next = (spread(x[0], SUB - 2) for x in (aa, bb, tt, dd))
    for section in range(SECTIONS):
        c, s = angles(alpha, beta, gamma)
        c_up, s_up = pltpu.roll(c, WIDTH - 1, 1), pltpu.roll(s, WIDTH - 1, 1)
        for v in range(section // SUB + 1):
            cc = pltpu.roll(c, SUB * v, 1, stride=1, stride_axis=0)
            ss = pltpu.roll(s, SUB * v, 1, stride=1, stride_axis=0)
            ru[v], rl[v] = cc * ru[v] - ss * rl[v], ss * ru[v] + cc * rl[v]
        if section == SECTIONS - 1:
            break
        moved = [pltpu.roll(x, 1, 0) for x in rl]
        rl = [jnp.where(sublane == 0, before, x) for before, x in zip([zero] + moved[:-1], moved)]
        a1, t1 = c * alpha - s * gamma, c * gamma - s * beta
        new_beta = s * (s * alpha + c * gamma) + c * (s * gamma + c * beta)
        alpha, beta, rest = c * a1 - s * t1, pltpu.roll(new_beta, WIDTH - 1, 1), s * a1 + c * t1
        b1, d1 = s_up * a_next + c_up * b_next, s_up * t_next + c_up * d_next
        gamma = c * b1 - s * d1
        if section == SECTIONS - 2:
            continue
        a1, t1 = c_up * a_next - s_up * b_next, c_up * t_next - s_up * d_next
        a_next = c * a1 - s * t1
        t_next, d_next = pltpu.roll(rest, WIDTH - 1, 1), pltpu.roll(s * b1 + c * d1, WIDTH - 1, 1)
        kept = (SECTIONS - 1 - section) // SUB + 1
        aa, bb, tt, dd = aa[:kept], bb[:kept], tt[:kept], dd[:kept]
        for v in range(kept):
            cc = pltpu.roll(c, BLK - SUB * (v + 1) + 1, 1, stride=1, stride_axis=0)
            ss = pltpu.roll(s, BLK - SUB * (v + 1) + 1, 1, stride=1, stride_axis=0)
            a1, b1 = cc * aa[v] - ss * bb[v], ss * aa[v] + cc * bb[v]
            t1, d1 = cc * tt[v] - ss * dd[v], ss * tt[v] + cc * dd[v]
            b2 = c * b1 - s * d1
            if v == 0:
                b_next = spread(b2, SUB - 3)
            aa[v], bb[v] = c * a1 - s * t1, pltpu.roll(b2, 1, 0)
            tt[v] = pltpu.roll(pltpu.roll(s * a1 + c * t1, WIDTH - 1, 1), SUB - 1, 0)
            dd[v] = pltpu.roll(s * b1 + c * d1, WIDTH - 1, 1)
        bb = [jnp.where(sublane == 0, after, x) for x, after in zip(bb, bb[1:] + [zero])]
        tt = [jnp.where(sublane == SUB - 1, before, x) for before, x in zip([gamma] + tt[:-1], tt)]
    for v in range(GROUPS):
        store[SUB * v:SUB * (v + 1), :] = ru[v]
        store[SECTIONS + SUB * v:SECTIONS + SUB * (v + 1), :] = rl[v]
    upper = (lanes & BLK) == 0
    diagonal = (rows - lanes + jnp.where(upper, 0, SECTIONS - 1)) & (BLK - 1)
    index = (diagonal & (SECTIONS - 1)) + jnp.where(upper, 0, SECTIONS)
    return jnp.where(diagonal < SECTIONS, jnp.take_along_axis(store[...].T, index, axis=1), 0.0)


def deal_kernel(assignment, stats, out, owners, slabs, sems):
    factors, _, order = stats.shape
    count = order // WIDTH
    copies = [pltpu.make_async_copy(stats.at[f], slabs.at[f], sems.at[f]) for f in range(factors)]
    for copy in copies:
        copy.start()
    table = pltpu.make_async_copy(assignment, owners, sems.at[factors])
    table.start()
    table.wait()
    for factor in range(factors):
        group = owners[factor]
        odd = group % 2 == 1
        base = group // 2 * (2 * count)
        copies[factor].wait()
        for place in range(count):
            home = base + jnp.where(odd, home_of(1, place, count), home_of(0, place, count))
            out[home] = slabs[factor, :, place * WIDTH:(place + 1) * WIDTH]


def pieces(x):
    high = x.astype(jnp.bfloat16)
    rest = x - high.astype(jnp.float32)
    middle = rest.astype(jnp.bfloat16)
    low = (rest - middle.astype(jnp.float32)).astype(jnp.bfloat16)
    return high, middle, low


def gram_of(parts, across):
    full = jnp.dot(jnp.concatenate(parts, axis=0), across, preferred_element_type=jnp.float32)
    crossed = full[2 * WIDTH:, :WIDTH]
    small = full[WIDTH:2 * WIDTH, WIDTH:] + (crossed + crossed.T)
    return full[:WIDTH, :WIDTH] + (full[:WIDTH, WIDTH:] + full[WIDTH:2 * WIDTH, :WIDTH] + small)


def apply(rotation, parts, near, far, start, exact):
    high, middle, low = pieces(rotation)
    first = jnp.concatenate(
        [jnp.concatenate([high, middle], axis=1), jnp.concatenate([middle, high], axis=1)], axis=0
    )
    last = jnp.concatenate([low, high], axis=1)
    total = parts[0].shape[1]
    for begin in range(0, total, CHUNK):
        end = min(begin + CHUNK, total)
        part = [x[:, begin:end] for x in parts]
        both = jnp.dot(first, jnp.concatenate(part[:2], axis=0), preferred_element_type=jnp.float32)
        small = both[WIDTH:]
        if exact:
            small = small + jnp.dot(
                last, jnp.concatenate([part[0], part[2]], axis=0), preferred_element_type=jnp.float32
            )
        post(near, far, pl.ds(start + begin, end - begin), both[:WIDTH] + small)


def swap_halves(x, axis, swapped):
    return jnp.where(swapped, pltpu.roll(x, BLK, axis), x)


def place_here():
    cell = lax.axis_index("jac")
    pair = 0
    for chain in CHAINS:
        for number, (x, z) in enumerate(chain):
            pair = jnp.where(cell == 4 * x + z, number, pair)
    return 2 * pair + lax.axis_index("fac") % 2


def leave_rotation(gram, store, place, swapped):
    rotation = small_rotation(gram, store, swapped).T
    bottom_first = jnp.logical_or(place == 0, place % 2 == 1)
    return swap_halves(rotation, 0, bottom_first)


def post(near, far, columns, block):
    near[:, columns] = block[:BLK]
    far[:, columns] = block[BLK:]


def first_kernel(work, far, near, store):
    place = place_here()
    order = work.shape[0]
    straight = work[...]
    parts = pieces(straight.T)
    across = jnp.concatenate(pieces(straight)[:2], axis=1)
    rotation = leave_rotation(gram_of(parts, across), store, place, False)
    apply(rotation, parts, near, far, 0, True)
    post(near, far, pl.ds(order, WIDTH), rotation)


def turned_pair(order, from_far, from_near, far, near, store, exact):
    place = place_here()
    swapped = place % 2 == 0
    parts = pieces(jnp.concatenate([from_near[:, :order], from_far[:, :order]], axis=0))
    across = jnp.concatenate(parts[:2], axis=0).T
    rotation = leave_rotation(gram_of(parts, across), store, place, swapped)
    rotation = swap_halves(rotation, 1, swapped)
    apply(rotation, parts, near, far, 0, exact)
    return rotation


def next_kernel(order, from_far, from_near, far, near, store):
    rotation = turned_pair(order, from_far, from_near, far, near, store, True)
    blank = jnp.zeros((BLK, WIDTH), jnp.float32)
    columns = [
        jnp.concatenate([from_near[:, order:], blank], axis=0),
        jnp.concatenate([blank, from_far[:, order:]], axis=0),
    ]
    apply(rotation, pieces(jnp.concatenate(columns, axis=1)), near, far, order, False)


def final_kernel(order, from_far, from_near, far, near, turn, store):
    turn[...] = turned_pair(order, from_far, from_near, far, near, store, False)


def final_basis(order, turn, from_far, from_near, far, near):
    blank = jnp.zeros((BLK, WIDTH), jnp.float32)
    first, second = pl.ds(order, WIDTH), pl.ds(order + WIDTH, WIDTH)
    columns = [
        jnp.concatenate([from_near[:, first], from_far[:, second]], axis=0),
        jnp.concatenate([from_near[:, second], blank], axis=0),
        jnp.concatenate([blank, from_far[:, first]], axis=0),
    ]
    apply(turn[...], pieces(jnp.concatenate(columns, axis=1)), near, far, 0, False)


def work_output(from_far, from_near, work, done, store, sems):
    done[...] = jnp.zeros_like(done)
    even = lax.axis_index("jac") % 2 == 0
    copies = []
    for number, begin in enumerate(range(0, work.shape[0], CHUNK)):
        rows = pl.ds(begin, CHUNK)
        near, far = from_near[:, rows], from_far[:, rows]
        pair = [jnp.where(even, far, near), jnp.where(even, near, far)]
        store[rows, :] = jnp.concatenate(pair, axis=0).T
        copies.append(pltpu.make_async_copy(store.at[rows], work.at[rows], sems.at[number]))
        copies[-1].start()
    for copy in copies:
        copy.wait()


def basis_output(from_far, from_near, after, basis):
    place = lax.axis_index("jac")
    count = lax.axis_size("jac")
    even = place % 2 == 0
    next_chip = far_place(place, count)
    rows = [
        [place ^ 1, next_chip, far_place(place ^ 1, count) ^ 1],
        [next_chip, far_place(next_chip ^ 1, count), far_place(next_chip, count) ^ 1],
    ]
    basis[...] = jnp.zeros_like(basis)
    left_half = lane_ids(WIDTH) < BLK
    for chunk in range(len(rows[0])):
        columns = pl.ds(chunk * WIDTH, WIDTH)
        piece = jnp.concatenate([from_near[:, columns], from_far[:, columns]], axis=0).T
        piece = swap_halves(piece, 1, even)
        for half in range(2):
            row = pl.multiple_of(rows[half][chunk] * WIDTH, WIDTH)
            left = jnp.logical_xor(even, half == 0)
            basis[pl.ds(row, WIDTH), :] += jnp.where(left_half == left, piece, 0.0)


def far_place(place, count):
    return jnp.clip(place + 2 * (place % 2) - 1, 0, count - 1)


def home_of(group, place, count):
    x, z = CHAINS[group % 2][place // 2]
    return (group // 2 * 2 + place % 2) * count + 4 * x + z


def routes(home, goal, factors, count):
    near, far = [], []
    for group in range(factors):
        for place in range(count):
            start = int(home[group * count + place])
            near.append((start, int(goal[group * count + (place ^ 1)])))
            other = min(max(place + 2 * (place % 2) - 1, 0), count - 1)
            far.append((start, int(goal[group * count + other])))
    return near, far


def vmem():
    return pl.BlockSpec(memory_space=pltpu.VMEM)


def hbm():
    return pl.BlockSpec(memory_space=pltpu.HBM)


MIB = 1024 * 1024
PARAMS = pltpu.CompilerParams(vmem_limit_bytes=40 * MIB)
DEAL_PARAMS = pltpu.CompilerParams(vmem_limit_bytes=62 * MIB + MIB // 2)


def shape(*dims):
    return jax.ShapeDtypeStruct(dims, jnp.float32)


def shards(statistics, assignment):
    factors, slab, order = statistics.shape
    count = order // WIDTH
    devices = factors * count
    axes = ("fac", "jac")
    home = np.array([home_of(g, p, count) for g in range(factors) for p in range(count)], np.int32)
    dealt = pl.pallas_call(
        deal_kernel,
        out_shape=shape(devices, slab, WIDTH),
        in_specs=[hbm(), hbm()],
        out_specs=vmem(),
        scratch_shapes=[
            pltpu.SMEM((factors,), jnp.int32),
            pltpu.VMEM((factors, slab, order), jnp.float32),
            pltpu.SemaphoreType.DMA((factors + 1,)),
        ],
        compiler_params=DEAL_PARAMS,
        name="deal",
    )(assignment, statistics)
    moved = lax.all_to_all(dealt, axes, split_axis=0, concat_axis=0, tiled=True)
    work = moved.reshape(order, WIDTH)
    store = pltpu.VMEM((WIDTH, WIDTH), jnp.float32)
    far, near = pl.pallas_call(
        first_kernel,
        out_shape=[shape(BLK, order + WIDTH)] * 2,
        in_specs=[vmem()],
        out_specs=[vmem()] * 2,
        scratch_shapes=[store],
        compiler_params=PARAMS,
        name="first_round",
    )(work)
    true_home = np.arange(devices, dtype=np.int32)
    for later in range(1, ROUNDS):
        near_route, far_route = routes(home, home, factors, count)
        from_far = lax.ppermute(far, axes, far_route)
        from_near = lax.ppermute(near, axes, near_route)
        if later < ROUNDS - 1:
            far, near = pl.pallas_call(
                functools.partial(next_kernel, order),
                out_shape=[shape(BLK, order + 2 * WIDTH)] * 2,
                in_specs=[vmem()] * 2,
                out_specs=[vmem()] * 2,
                scratch_shapes=[store],
                compiler_params=PARAMS,
                name="next_round",
            )(from_far, from_near)
    far, near, turn = pl.pallas_call(
        functools.partial(final_kernel, order),
        out_shape=[shape(BLK, order), shape(BLK, order), shape(WIDTH, WIDTH)],
        in_specs=[vmem()] * 2,
        out_specs=[vmem()] * 3,
        scratch_shapes=[store],
        compiler_params=PARAMS,
        name="final_round",
    )(from_far, from_near)
    far_basis, near_basis = pl.pallas_call(
        functools.partial(final_basis, order),
        out_shape=[shape(BLK, ROUNDS * WIDTH)] * 2,
        in_specs=[vmem()] * 3,
        out_specs=[vmem()] * 2,
        compiler_params=PARAMS,
        name="final_basis",
    )(turn, from_far, from_near)
    near_route, far_route = routes(home, true_home, factors, count)
    from_far = lax.ppermute(far, axes, far_route)
    from_near = lax.ppermute(near, axes, near_route)
    from_far_basis = lax.ppermute(far_basis, axes, far_route)
    from_near_basis = lax.ppermute(near_basis, axes, near_route)
    work, done = pl.pallas_call(
        work_output,
        out_shape=[shape(order, WIDTH), shape(SUB, WIDTH)],
        in_specs=[vmem()] * 2,
        out_specs=[hbm(), vmem()],
        scratch_shapes=[pltpu.VMEM((order, WIDTH), jnp.float32), pltpu.SemaphoreType.DMA((order // CHUNK,))],
        compiler_params=PARAMS,
        name="work_output",
    )(from_far, from_near)
    basis = pl.pallas_call(
        basis_output,
        out_shape=shape(order, WIDTH),
        in_specs=[vmem()] * 3,
        out_specs=vmem(),
        compiler_params=PARAMS,
        name="basis_output",
    )(from_far_basis, from_near_basis, done)
    return work[None], basis[None]


def solution(mesh):
    return jax.shard_map(
        shards,
        mesh=mesh,
        in_specs=(P(None, ("fac", "jac"), None), P()),
        out_specs=(P("fac", None, "jac"), P("fac", None, "jac")),
        check_vma=False,
    )
```

```python
import functools

import jax
import jax.numpy as jnp
import numpy as np
from jax import lax
from jax.experimental import pallas as pl
from jax.experimental.pallas import tpu as pltpu
from jax.sharding import PartitionSpec as P

ROUNDS = 3
CHUNK = 256
PIECE = 512
CHAINS = (
    ((0, 1), (0, 0), (1, 3), (1, 2), (2, 1), (2, 0), (3, 3), (3, 2)),
    ((0, 3), (0, 2), (1, 1), (1, 0), (2, 3), (2, 2), (3, 1), (3, 0)),
)
BLK = 64
WIDTH = 2 * BLK
SECTIONS = 16
SUB = 8
GROUPS = SECTIONS // SUB


def lane_ids(rows):
    return lax.broadcasted_iota(jnp.int32, (rows, WIDTH), 1)


def angles(alpha, beta, gamma):
    diff = beta - alpha
    square = diff * diff + 4.0 * gamma * gamma
    inverse = jnp.where(square > 0, lax.rsqrt(square), 0.0)
    along = diff * inverse
    lead = 1.0 + jnp.abs(along)
    cross = (2.0 * gamma) * inverse * along
    scale = lax.rsqrt(lead * lead + cross * cross)
    c, s = lead * scale, cross * scale
    short = (1.0 - c * c) - s * s
    return c + short * (0.5 * c), s + short * (0.5 * s)


def small_rotation(gram, store, swapped):
    lanes = lane_ids(WIDTH)
    rows = lax.broadcasted_iota(jnp.int32, (WIDTH, WIDTH), 0)
    reach = SECTIONS - 1 - (lanes & (SECTIONS - 1))
    skew = ((rows + reach) & (BLK - 1)) + jnp.where((lanes & SECTIONS) == 0, 0, BLK)
    store[...] = jnp.take_along_axis(gram, skew, axis=1).T
    low = lane_ids(SUB) < BLK
    sublane = lax.broadcasted_iota(jnp.int32, (SUB, WIDTH), 0)
    aa, bb, tt, dd = [], [], [], []
    for v in range(GROUPS):
        begin = SECTIONS - SUB * (v + 1)
        top, bot = store[begin:begin + SUB, :], store[SECTIONS + begin:SECTIONS + begin + SUB, :]
        top_swap, bot_swap = pltpu.roll(top, BLK, 1), pltpu.roll(bot, BLK, 1)
        blocks = (
            jnp.where(low, top, top_swap),
            jnp.where(low, bot, bot_swap),
            jnp.where(low, top_swap, top),
            jnp.where(low, bot_swap, bot),
        )
        aa.append(jnp.where(swapped, blocks[3], blocks[0]))
        bb.append(jnp.where(swapped, blocks[2], blocks[1]))
        tt.append(jnp.where(swapped, blocks[1], blocks[2]))
        dd.append(jnp.where(swapped, blocks[0], blocks[3]))
    start = jnp.where(sublane == 0, 1.0, 0.0).astype(jnp.float32)
    zero = jnp.zeros((SUB, WIDTH), jnp.float32)
    ru = [jnp.where(low, start, 0.0)] + [zero] * (GROUPS - 1)
    rl = [jnp.where(low, 0.0, start)] + [zero] * (GROUPS - 1)

    def spread(x, row):
        return jnp.broadcast_to(x[row:row + 1], (SUB, WIDTH))

    alpha, beta, gamma = (spread(x[0], SUB - 1) for x in (aa, dd, bb))
    a_next, b_next, t_next, d_next = (spread(x[0], SUB - 2) for x in (aa, bb, tt, dd))
    for section in range(SECTIONS):
        c, s = angles(alpha, beta, gamma)
        c_up, s_up = pltpu.roll(c, WIDTH - 1, 1), pltpu.roll(s, WIDTH - 1, 1)
        for v in range(section // SUB + 1):
            cc = pltpu.roll(c, SUB * v, 1, stride=1, stride_axis=0)
            ss = pltpu.roll(s, SUB * v, 1, stride=1, stride_axis=0)
            ru[v], rl[v] = cc * ru[v] - ss * rl[v], ss * ru[v] + cc * rl[v]
        if section == SECTIONS - 1:
            break
        moved = [pltpu.roll(x, 1, 0) for x in rl]
        rl = [jnp.where(sublane == 0, before, x) for before, x in zip([zero] + moved[:-1], moved)]
        a1, t1 = c * alpha - s * gamma, c * gamma - s * beta
        new_beta = s * (s * alpha + c * gamma) + c * (s * gamma + c * beta)
        alpha, beta, rest = c * a1 - s * t1, pltpu.roll(new_beta, WIDTH - 1, 1), s * a1 + c * t1
        b1, d1 = s_up * a_next + c_up * b_next, s_up * t_next + c_up * d_next
        gamma = c * b1 - s * d1
        if section == SECTIONS - 2:
            continue
        a1, t1 = c_up * a_next - s_up * b_next, c_up * t_next - s_up * d_next
        a_next = c * a1 - s * t1
        t_next, d_next = pltpu.roll(rest, WIDTH - 1, 1), pltpu.roll(s * b1 + c * d1, WIDTH - 1, 1)
        kept = (SECTIONS - 1 - section) // SUB + 1
        aa, bb, tt, dd = aa[:kept], bb[:kept], tt[:kept], dd[:kept]
        for v in range(kept):
            cc = pltpu.roll(c, BLK - SUB * (v + 1) + 1, 1, stride=1, stride_axis=0)
            ss = pltpu.roll(s, BLK - SUB * (v + 1) + 1, 1, stride=1, stride_axis=0)
            a1, b1 = cc * aa[v] - ss * bb[v], ss * aa[v] + cc * bb[v]
            t1, d1 = cc * tt[v] - ss * dd[v], ss * tt[v] + cc * dd[v]
            b2 = c * b1 - s * d1
            if v == 0:
                b_next = spread(b2, SUB - 3)
            aa[v], bb[v] = c * a1 - s * t1, pltpu.roll(b2, 1, 0)
            tt[v] = pltpu.roll(pltpu.roll(s * a1 + c * t1, WIDTH - 1, 1), SUB - 1, 0)
            dd[v] = pltpu.roll(s * b1 + c * d1, WIDTH - 1, 1)
        bb = [jnp.where(sublane == 0, after, x) for x, after in zip(bb, bb[1:] + [zero])]
        tt = [jnp.where(sublane == SUB - 1, before, x) for before, x in zip([gamma] + tt[:-1], tt)]
    for v in range(GROUPS):
        store[SUB * v:SUB * (v + 1), :] = ru[v]
        store[SECTIONS + SUB * v:SECTIONS + SUB * (v + 1), :] = rl[v]
    upper = (lanes & BLK) == 0
    diagonal = (rows - lanes + jnp.where(upper, 0, SECTIONS - 1)) & (BLK - 1)
    index = (diagonal & (SECTIONS - 1)) + jnp.where(upper, 0, SECTIONS)
    return jnp.where(diagonal < SECTIONS, jnp.take_along_axis(store[...].T, index, axis=1), 0.0)


def deal_kernel(assignment, stats, out, owners, slabs, sems):
    factors, _, order = stats.shape
    count = order // WIDTH
    copies = [pltpu.make_async_copy(stats.at[f], slabs.at[f], sems.at[f]) for f in range(factors)]
    for copy in copies:
        copy.start()
    table = pltpu.make_async_copy(assignment, owners, sems.at[factors])
    table.start()
    table.wait()
    for factor in range(factors):
        group = owners[factor]
        odd = group % 2 == 1
        base = group // 2 * (2 * count)
        copies[factor].wait()
        for place in range(count):
            home = base + jnp.where(odd, home_of(1, place, count), home_of(0, place, count))
            out[home] = slabs[factor, :, place * WIDTH:(place + 1) * WIDTH]


def pieces(x):
    high = x.astype(jnp.bfloat16)
    rest = x - high.astype(jnp.float32)
    middle = rest.astype(jnp.bfloat16)
    low = (rest - middle.astype(jnp.float32)).astype(jnp.bfloat16)
    return high, middle, low


def gram_of(parts, across):
    full = jnp.dot(jnp.concatenate(parts, axis=0), across, preferred_element_type=jnp.float32)
    crossed = full[2 * WIDTH:, :WIDTH]
    small = full[WIDTH:2 * WIDTH, WIDTH:] + (crossed + crossed.T)
    return full[:WIDTH, :WIDTH] + (full[:WIDTH, WIDTH:] + full[WIDTH:2 * WIDTH, :WIDTH] + small)


def apply(rotation, parts, near, far, start, exact):
    high, middle, low = pieces(rotation)
    first = jnp.concatenate(
        [jnp.concatenate([high, middle], axis=1), jnp.concatenate([middle, high], axis=1)], axis=0
    )
    last = jnp.concatenate([low, high], axis=1)
    total = parts[0].shape[1]
    for begin in range(0, total, CHUNK):
        end = min(begin + CHUNK, total)
        part = [x[:, begin:end] for x in parts]
        both = jnp.dot(first, jnp.concatenate(part[:2], axis=0), preferred_element_type=jnp.float32)
        small = both[WIDTH:]
        if exact:
            small = small + jnp.dot(
                last, jnp.concatenate([part[0], part[2]], axis=0), preferred_element_type=jnp.float32
            )
        post(near, far, pl.ds(start + begin, end - begin), both[:WIDTH] + small)


def swap_halves(x, axis, swapped):
    return jnp.where(swapped, pltpu.roll(x, BLK, axis), x)


def place_here():
    cell = lax.axis_index("jac")
    pair = 0
    for chain in CHAINS:
        for number, (x, z) in enumerate(chain):
            pair = jnp.where(cell == 4 * x + z, number, pair)
    return 2 * pair + lax.axis_index("fac") % 2


def leave_rotation(gram, store, place, swapped):
    rotation = small_rotation(gram, store, swapped).T
    bottom_first = jnp.logical_or(place == 0, place % 2 == 1)
    return swap_halves(rotation, 0, bottom_first)


def post(near, far, columns, block):
    near[:, columns] = block[:BLK]
    far[:, columns] = block[BLK:]


def first_kernel(work, far, near, store):
    place = place_here()
    order = work.shape[0]
    straight = work[...]
    parts = pieces(straight.T)
    across = jnp.concatenate(pieces(straight)[:2], axis=1)
    rotation = leave_rotation(gram_of(parts, across), store, place, False)
    apply(rotation, parts, near, far, 0, True)
    post(near, far, pl.ds(order, WIDTH), rotation)


def turned_pair(order, from_far, from_near, far, near, store, exact):
    place = place_here()
    swapped = place % 2 == 0
    parts = pieces(jnp.concatenate([from_near[:, :order], from_far[:, :order]], axis=0))
    across = jnp.concatenate(parts[:2], axis=0).T
    rotation = leave_rotation(gram_of(parts, across), store, place, swapped)
    rotation = swap_halves(rotation, 1, swapped)
    apply(rotation, parts, near, far, 0, exact)
    return rotation


def next_kernel(order, from_far, from_near, far, near, store):
    rotation = turned_pair(order, from_far, from_near, far, near, store, True)
    blank = jnp.zeros((BLK, WIDTH), jnp.float32)
    columns = [
        jnp.concatenate([from_near[:, order:], blank], axis=0),
        jnp.concatenate([blank, from_far[:, order:]], axis=0),
    ]
    apply(rotation, pieces(jnp.concatenate(columns, axis=1)), near, far, order, False)


def final_kernel(order, from_far, from_near, far, near, turn, store):
    turn[...] = turned_pair(order, from_far, from_near, far, near, store, False)


def final_basis(order, turn, from_far, from_near, far, near):
    blank = jnp.zeros((BLK, WIDTH), jnp.float32)
    first, second = pl.ds(order, WIDTH), pl.ds(order + WIDTH, WIDTH)
    columns = [
        jnp.concatenate([from_near[:, first], from_far[:, second]], axis=0),
        jnp.concatenate([from_near[:, second], blank], axis=0),
        jnp.concatenate([blank, from_far[:, first]], axis=0),
    ]
    apply(turn[...], pieces(jnp.concatenate(columns, axis=1)), near, far, 0, False)


def work_output(from_far, from_near, after, work, store, sems):
    even = lax.axis_index("jac") % 2 == 0
    copies = []
    for number, begin in enumerate(range(0, work.shape[0], PIECE)):
        rows = pl.ds(begin, PIECE)
        near, far = from_near[:, rows], from_far[:, rows]
        pair = [jnp.where(even, far, near), jnp.where(even, near, far)]
        store[rows, :] = jnp.concatenate(pair, axis=0).T
        copies.append(pltpu.make_async_copy(store.at[rows], work.at[rows], sems.at[number]))
        copies[-1].start()
    for copy in copies:
        copy.wait()


def basis_output(from_far, from_near, basis, done):
    done[...] = jnp.zeros_like(done)
    place = lax.axis_index("jac")
    count = lax.axis_size("jac")
    even = place % 2 == 0
    next_chip = far_place(place, count)
    rows = [
        [place ^ 1, next_chip, far_place(place ^ 1, count) ^ 1],
        [next_chip, far_place(next_chip ^ 1, count), far_place(next_chip, count) ^ 1],
    ]
    basis[...] = jnp.zeros_like(basis)
    left_half = lane_ids(WIDTH) < BLK
    for chunk in range(len(rows[0])):
        columns = pl.ds(chunk * WIDTH, WIDTH)
        piece = jnp.concatenate([from_near[:, columns], from_far[:, columns]], axis=0).T
        piece = swap_halves(piece, 1, even)
        for half in range(2):
            row = pl.multiple_of(rows[half][chunk] * WIDTH, WIDTH)
            left = jnp.logical_xor(even, half == 0)
            basis[pl.ds(row, WIDTH), :] += jnp.where(left_half == left, piece, 0.0)


def far_place(place, count):
    return jnp.clip(place + 2 * (place % 2) - 1, 0, count - 1)


def home_of(group, place, count):
    x, z = CHAINS[group % 2][place // 2]
    return (group // 2 * 2 + place % 2) * count + 4 * x + z


def routes(home, goal, factors, count):
    near, far = [], []
    for group in range(factors):
        for place in range(count):
            start = int(home[group * count + place])
            near.append((start, int(goal[group * count + (place ^ 1)])))
            other = min(max(place + 2 * (place % 2) - 1, 0), count - 1)
            far.append((start, int(goal[group * count + other])))
    return near, far


def vmem():
    return pl.BlockSpec(memory_space=pltpu.VMEM)


def hbm():
    return pl.BlockSpec(memory_space=pltpu.HBM)


MIB = 1024 * 1024
PARAMS = pltpu.CompilerParams(vmem_limit_bytes=40 * MIB)
DEAL_PARAMS = pltpu.CompilerParams(vmem_limit_bytes=62 * MIB + MIB // 2)


def shape(*dims):
    return jax.ShapeDtypeStruct(dims, jnp.float32)


def shards(statistics, assignment):
    factors, slab, order = statistics.shape
    count = order // WIDTH
    devices = factors * count
    axes = ("fac", "jac")
    home = np.array([home_of(g, p, count) for g in range(factors) for p in range(count)], np.int32)
    dealt = pl.pallas_call(
        deal_kernel,
        out_shape=shape(devices, slab, WIDTH),
        in_specs=[hbm(), hbm()],
        out_specs=vmem(),
        scratch_shapes=[
            pltpu.SMEM((factors,), jnp.int32),
            pltpu.VMEM((factors, slab, order), jnp.float32),
            pltpu.SemaphoreType.DMA((factors + 1,)),
        ],
        compiler_params=DEAL_PARAMS,
        name="deal",
    )(assignment, statistics)
    moved = lax.all_to_all(dealt, axes, split_axis=0, concat_axis=0, tiled=True)
    work = moved.reshape(order, WIDTH)
    store = pltpu.VMEM((WIDTH, WIDTH), jnp.float32)
    far, near = pl.pallas_call(
        first_kernel,
        out_shape=[shape(BLK, order + WIDTH)] * 2,
        in_specs=[vmem()],
        out_specs=[vmem()] * 2,
        scratch_shapes=[store],
        compiler_params=PARAMS,
        name="first_round",
    )(work)
    true_home = np.arange(devices, dtype=np.int32)
    for later in range(1, ROUNDS):
        near_route, far_route = routes(home, home, factors, count)
        from_far = lax.ppermute(far, axes, far_route)
        from_near = lax.ppermute(near, axes, near_route)
        if later < ROUNDS - 1:
            far, near = pl.pallas_call(
                functools.partial(next_kernel, order),
                out_shape=[shape(BLK, order + 2 * WIDTH)] * 2,
                in_specs=[vmem()] * 2,
                out_specs=[vmem()] * 2,
                scratch_shapes=[store],
                compiler_params=PARAMS,
                name="next_round",
            )(from_far, from_near)
    far, near, turn = pl.pallas_call(
        functools.partial(final_kernel, order),
        out_shape=[shape(BLK, order), shape(BLK, order), shape(WIDTH, WIDTH)],
        in_specs=[vmem()] * 2,
        out_specs=[vmem()] * 3,
        scratch_shapes=[store],
        compiler_params=PARAMS,
        name="final_round",
    )(from_far, from_near)
    far_basis, near_basis = pl.pallas_call(
        functools.partial(final_basis, order),
        out_shape=[shape(BLK, ROUNDS * WIDTH)] * 2,
        in_specs=[vmem()] * 3,
        out_specs=[vmem()] * 2,
        compiler_params=PARAMS,
        name="final_basis",
    )(turn, from_far, from_near)
    near_route, far_route = routes(home, true_home, factors, count)
    from_far = lax.ppermute(far, axes, far_route)
    from_near = lax.ppermute(near, axes, near_route)
    from_far_basis = lax.ppermute(far_basis, axes, far_route)
    from_near_basis = lax.ppermute(near_basis, axes, near_route)
    basis, done = pl.pallas_call(
        basis_output,
        out_shape=[shape(order, WIDTH), shape(SUB, WIDTH)],
        in_specs=[vmem()] * 2,
        out_specs=[vmem()] * 2,
        compiler_params=PARAMS,
        name="basis_output",
    )(from_far_basis, from_near_basis)
    work = pl.pallas_call(
        work_output,
        out_shape=shape(order, WIDTH),
        in_specs=[vmem()] * 3,
        out_specs=hbm(),
        scratch_shapes=[pltpu.VMEM((order, WIDTH), jnp.float32), pltpu.SemaphoreType.DMA((order // PIECE,))],
        compiler_params=PARAMS,
        name="work_output",
    )(from_far, from_near, done)
    return work[None], basis[None]


def solution(mesh):
    return jax.shard_map(
        shards,
        mesh=mesh,
        in_specs=(P(None, ("fac", "jac"), None), P()),
        out_specs=(P("fac", None, "jac"), P("fac", None, "jac")),
        check_vma=False,
    )
```

```python
import functools

import jax
import jax.numpy as jnp
import numpy as np
from jax import lax
from jax.experimental import pallas as pl
from jax.experimental.pallas import tpu as pltpu
from jax.sharding import PartitionSpec as P

ROUNDS = 3
CHUNK = 512
CHAINS = (
    ((0, 1), (0, 0), (1, 3), (1, 2), (2, 1), (2, 0), (3, 3), (3, 2)),
    ((0, 3), (0, 2), (1, 1), (1, 0), (2, 3), (2, 2), (3, 1), (3, 0)),
)
BLK = 64
WIDTH = 2 * BLK
SECTIONS = 16
SUB = 8
GROUPS = SECTIONS // SUB


def lane_ids(rows):
    return lax.broadcasted_iota(jnp.int32, (rows, WIDTH), 1)


def angles(alpha, beta, gamma):
    diff = beta - alpha
    square = diff * diff + 4.0 * gamma * gamma
    inverse = jnp.where(square > 0, lax.rsqrt(square), 0.0)
    along = diff * inverse
    lead = 1.0 + jnp.abs(along)
    cross = (2.0 * gamma) * inverse * along
    scale = lax.rsqrt(lead * lead + cross * cross)
    c, s = lead * scale, cross * scale
    short = (1.0 - c * c) - s * s
    return c + short * (0.5 * c), s + short * (0.5 * s)


def small_rotation(gram, store, swapped):
    lanes = lane_ids(WIDTH)
    rows = lax.broadcasted_iota(jnp.int32, (WIDTH, WIDTH), 0)
    reach = SECTIONS - 1 - (lanes & (SECTIONS - 1))
    skew = ((rows + reach) & (BLK - 1)) + jnp.where((lanes & SECTIONS) == 0, 0, BLK)
    store[...] = jnp.take_along_axis(gram, skew, axis=1).T
    low = lane_ids(SUB) < BLK
    sublane = lax.broadcasted_iota(jnp.int32, (SUB, WIDTH), 0)
    aa, bb, tt, dd = [], [], [], []
    for v in range(GROUPS):
        begin = SECTIONS - SUB * (v + 1)
        top, bot = store[begin:begin + SUB, :], store[SECTIONS + begin:SECTIONS + begin + SUB, :]
        top_swap, bot_swap = pltpu.roll(top, BLK, 1), pltpu.roll(bot, BLK, 1)
        blocks = (
            jnp.where(low, top, top_swap),
            jnp.where(low, bot, bot_swap),
            jnp.where(low, top_swap, top),
            jnp.where(low, bot_swap, bot),
        )
        aa.append(jnp.where(swapped, blocks[3], blocks[0]))
        bb.append(jnp.where(swapped, blocks[2], blocks[1]))
        tt.append(jnp.where(swapped, blocks[1], blocks[2]))
        dd.append(jnp.where(swapped, blocks[0], blocks[3]))
    start = jnp.where(sublane == 0, 1.0, 0.0).astype(jnp.float32)
    zero = jnp.zeros((SUB, WIDTH), jnp.float32)
    ru = [jnp.where(low, start, 0.0)] + [zero] * (GROUPS - 1)
    rl = [jnp.where(low, 0.0, start)] + [zero] * (GROUPS - 1)

    def spread(x, row):
        return jnp.broadcast_to(x[row:row + 1], (SUB, WIDTH))

    alpha, beta, gamma = (spread(x[0], SUB - 1) for x in (aa, dd, bb))
    a_next, b_next, t_next, d_next = (spread(x[0], SUB - 2) for x in (aa, bb, tt, dd))
    for section in range(SECTIONS):
        c, s = angles(alpha, beta, gamma)
        c_up, s_up = pltpu.roll(c, WIDTH - 1, 1), pltpu.roll(s, WIDTH - 1, 1)
        for v in range(section // SUB + 1):
            cc = pltpu.roll(c, SUB * v, 1, stride=1, stride_axis=0)
            ss = pltpu.roll(s, SUB * v, 1, stride=1, stride_axis=0)
            ru[v], rl[v] = cc * ru[v] - ss * rl[v], ss * ru[v] + cc * rl[v]
        if section == SECTIONS - 1:
            break
        moved = [pltpu.roll(x, 1, 0) for x in rl]
        rl = [jnp.where(sublane == 0, before, x) for before, x in zip([zero] + moved[:-1], moved)]
        a1, t1 = c * alpha - s * gamma, c * gamma - s * beta
        new_beta = s * (s * alpha + c * gamma) + c * (s * gamma + c * beta)
        alpha, beta, rest = c * a1 - s * t1, pltpu.roll(new_beta, WIDTH - 1, 1), s * a1 + c * t1
        b1, d1 = s_up * a_next + c_up * b_next, s_up * t_next + c_up * d_next
        gamma = c * b1 - s * d1
        if section == SECTIONS - 2:
            continue
        a1, t1 = c_up * a_next - s_up * b_next, c_up * t_next - s_up * d_next
        a_next = c * a1 - s * t1
        t_next, d_next = pltpu.roll(rest, WIDTH - 1, 1), pltpu.roll(s * b1 + c * d1, WIDTH - 1, 1)
        kept = (SECTIONS - 1 - section) // SUB + 1
        aa, bb, tt, dd = aa[:kept], bb[:kept], tt[:kept], dd[:kept]
        for v in range(kept):
            cc = pltpu.roll(c, BLK - SUB * (v + 1) + 1, 1, stride=1, stride_axis=0)
            ss = pltpu.roll(s, BLK - SUB * (v + 1) + 1, 1, stride=1, stride_axis=0)
            a1, b1 = cc * aa[v] - ss * bb[v], ss * aa[v] + cc * bb[v]
            t1, d1 = cc * tt[v] - ss * dd[v], ss * tt[v] + cc * dd[v]
            b2 = c * b1 - s * d1
            if v == 0:
                b_next = spread(b2, SUB - 3)
            aa[v], bb[v] = c * a1 - s * t1, pltpu.roll(b2, 1, 0)
            tt[v] = pltpu.roll(pltpu.roll(s * a1 + c * t1, WIDTH - 1, 1), SUB - 1, 0)
            dd[v] = pltpu.roll(s * b1 + c * d1, WIDTH - 1, 1)
        bb = [jnp.where(sublane == 0, after, x) for x, after in zip(bb, bb[1:] + [zero])]
        tt = [jnp.where(sublane == SUB - 1, before, x) for before, x in zip([gamma] + tt[:-1], tt)]
    for v in range(GROUPS):
        store[SUB * v:SUB * (v + 1), :] = ru[v]
        store[SECTIONS + SUB * v:SECTIONS + SUB * (v + 1), :] = rl[v]
    upper = (lanes & BLK) == 0
    diagonal = (rows - lanes + jnp.where(upper, 0, SECTIONS - 1)) & (BLK - 1)
    index = (diagonal & (SECTIONS - 1)) + jnp.where(upper, 0, SECTIONS)
    return jnp.where(diagonal < SECTIONS, jnp.take_along_axis(store[...].T, index, axis=1), 0.0)


def deal_kernel(assignment, stats, out, owners, slabs, sems):
    factors, _, order = stats.shape
    count = order // WIDTH
    copies = [pltpu.make_async_copy(stats.at[f], slabs.at[f], sems.at[f]) for f in range(factors)]
    for copy in copies:
        copy.start()
    table = pltpu.make_async_copy(assignment, owners, sems.at[factors])
    table.start()
    table.wait()
    for factor in range(factors):
        group = owners[factor]
        odd = group % 2 == 1
        base = group // 2 * (2 * count)
        copies[factor].wait()
        for place in range(count):
            home = base + jnp.where(odd, home_of(1, place, count), home_of(0, place, count))
            out[home] = slabs[factor, :, place * WIDTH:(place + 1) * WIDTH]


def pieces(x):
    high = x.astype(jnp.bfloat16)
    rest = x - high.astype(jnp.float32)
    middle = rest.astype(jnp.bfloat16)
    low = (rest - middle.astype(jnp.float32)).astype(jnp.bfloat16)
    return high, middle, low


def gram_of(parts, across):
    full = jnp.dot(jnp.concatenate(parts, axis=0), across, preferred_element_type=jnp.float32)
    crossed = full[2 * WIDTH:, :WIDTH]
    small = full[WIDTH:2 * WIDTH, WIDTH:] + (crossed + crossed.T)
    return full[:WIDTH, :WIDTH] + (full[:WIDTH, WIDTH:] + full[WIDTH:2 * WIDTH, :WIDTH] + small)


def apply(rotation, parts, near, far, start, exact):
    high, middle, low = pieces(rotation)
    first = jnp.concatenate(
        [jnp.concatenate([high, middle], axis=1), jnp.concatenate([middle, high], axis=1)], axis=0
    )
    last = jnp.concatenate([low, high], axis=1)
    total = parts[0].shape[1]
    for begin in range(0, total, CHUNK):
        end = min(begin + CHUNK, total)
        part = [x[:, begin:end] for x in parts]
        both = jnp.dot(first, jnp.concatenate(part[:2], axis=0), preferred_element_type=jnp.float32)
        small = both[WIDTH:]
        if exact:
            small = small + jnp.dot(
                last, jnp.concatenate([part[0], part[2]], axis=0), preferred_element_type=jnp.float32
            )
        post(near, far, pl.ds(start + begin, end - begin), both[:WIDTH] + small)


def swap_halves(x, axis, swapped):
    return jnp.where(swapped, pltpu.roll(x, BLK, axis), x)


def place_here():
    cell = lax.axis_index("jac")
    pair = 0
    for chain in CHAINS:
        for number, (x, z) in enumerate(chain):
            pair = jnp.where(cell == 4 * x + z, number, pair)
    return 2 * pair + lax.axis_index("fac") % 2


def leave_rotation(gram, store, place, swapped):
    rotation = small_rotation(gram, store, swapped).T
    bottom_first = jnp.logical_or(place == 0, place % 2 == 1)
    return swap_halves(rotation, 0, bottom_first)


def post(near, far, columns, block):
    near[:, columns] = block[:BLK]
    far[:, columns] = block[BLK:]


def first_kernel(work, far, near, store):
    place = place_here()
    order = work.shape[0]
    straight = work[...]
    parts = pieces(straight.T)
    across = jnp.concatenate(pieces(straight)[:2], axis=1)
    rotation = leave_rotation(gram_of(parts, across), store, place, False)
    apply(rotation, parts, near, far, 0, True)
    post(near, far, pl.ds(order, WIDTH), rotation)


def next_kernel(order, final, from_far, from_near, far, near, store):
    place = place_here()
    swapped = place % 2 == 0
    parts = pieces(jnp.concatenate([from_near[:, :order], from_far[:, :order]], axis=0))
    across = jnp.concatenate(parts[:2], axis=0).T
    rotation = leave_rotation(gram_of(parts, across), store, place, swapped)
    rotation = swap_halves(rotation, 1, swapped)
    apply(rotation, parts, near, far, 0, not final)
    blank = jnp.zeros((BLK, WIDTH), jnp.float32)
    near_basis = [from_near[:, c:c + WIDTH] for c in range(order, from_near.shape[1], WIDTH)]
    far_basis = [from_far[:, c:c + WIDTH] for c in range(order, from_far.shape[1], WIDTH)]
    if final:
        near_basis, far_basis = near_basis + [blank], [far_basis[1], blank, far_basis[0]]
    else:
        near_basis, far_basis = near_basis + [blank], [blank] + far_basis
    columns = [jnp.concatenate(halves, axis=0) for halves in zip(near_basis, far_basis)]
    apply(rotation, pieces(jnp.concatenate(columns, axis=1)), near, far, order, False)


def last_kernel(from_far, from_near, work, basis, work_store, basis_store, sems):
    order = work.shape[0]
    place = lax.axis_index("jac")
    count = lax.axis_size("jac")
    next_chip = far_place(place, count)
    rows = [
        [place ^ 1, next_chip, far_place(place ^ 1, count) ^ 1],
        [next_chip, far_place(next_chip ^ 1, count), far_place(next_chip, count) ^ 1],
    ]
    even = place % 2 == 0
    basis_store[...] = jnp.zeros_like(basis_store)
    chunks = (from_near.shape[1] - order) // WIDTH
    left_half = lane_ids(WIDTH) < BLK
    for chunk in range(chunks):
        columns = pl.ds(order + chunk * WIDTH, WIDTH)
        piece = jnp.concatenate([from_near[:, columns], from_far[:, columns]], axis=0).T
        piece = swap_halves(piece, 1, even)
        for half in range(2):
            row = pl.multiple_of(rows[half][chunk] * WIDTH, WIDTH)
            left = jnp.logical_xor(even, half == 0)
            basis_store[pl.ds(row, WIDTH), :] += jnp.where(left_half == left, piece, 0.0)
    copies = [pltpu.make_async_copy(basis_store, basis, sems.at[0])]
    copies[0].start()
    for number, begin in enumerate(range(0, order, CHUNK)):
        rows = pl.ds(begin, CHUNK)
        near, far = from_near[:, rows], from_far[:, rows]
        pair = [jnp.where(even, far, near), jnp.where(even, near, far)]
        work_store[rows, :] = jnp.concatenate(pair, axis=0).T
        copies.append(pltpu.make_async_copy(work_store.at[rows], work.at[rows], sems.at[number + 1]))
        copies[-1].start()
    for copy in copies:
        copy.wait()


def far_place(place, count):
    return jnp.clip(place + 2 * (place % 2) - 1, 0, count - 1)


def home_of(group, place, count):
    x, z = CHAINS[group % 2][place // 2]
    return (group // 2 * 2 + place % 2) * count + 4 * x + z


def vmem():
    return pl.BlockSpec(memory_space=pltpu.VMEM)


def hbm():
    return pl.BlockSpec(memory_space=pltpu.HBM)


MIB = 1024 * 1024
PARAMS = pltpu.CompilerParams(vmem_limit_bytes=40 * MIB)
DEAL_PARAMS = pltpu.CompilerParams(vmem_limit_bytes=62 * MIB + MIB // 2)


def shape(*dims):
    return jax.ShapeDtypeStruct(dims, jnp.float32)


def shards(statistics, assignment):
    factors, slab, order = statistics.shape
    count = order // WIDTH
    devices = factors * count
    axes = ("fac", "jac")
    home = np.array([home_of(g, p, count) for g in range(factors) for p in range(count)], np.int32)
    dealt = pl.pallas_call(
        deal_kernel,
        out_shape=shape(devices, slab, WIDTH),
        in_specs=[hbm(), hbm()],
        out_specs=vmem(),
        scratch_shapes=[
            pltpu.SMEM((factors,), jnp.int32),
            pltpu.VMEM((factors, slab, order), jnp.float32),
            pltpu.SemaphoreType.DMA((factors + 1,)),
        ],
        compiler_params=DEAL_PARAMS,
        name="deal",
    )(assignment, statistics)
    moved = lax.all_to_all(dealt, axes, split_axis=0, concat_axis=0, tiled=True)
    work = moved.reshape(order, WIDTH)
    store = pltpu.VMEM((WIDTH, WIDTH), jnp.float32)
    far, near = pl.pallas_call(
        first_kernel,
        out_shape=[shape(BLK, order + WIDTH)] * 2,
        in_specs=[vmem()],
        out_specs=[vmem()] * 2,
        scratch_shapes=[store],
        compiler_params=PARAMS,
        name="first_round",
    )(work)
    for later in range(1, ROUNDS + 1):
        goal = home if later < ROUNDS else np.arange(devices, dtype=np.int32)
        near_route, far_route = [], []
        for group in range(factors):
            for place in range(count):
                start = int(home[group * count + place])
                near_route.append((start, int(goal[group * count + (place ^ 1)])))
                other = min(max(place + 2 * (place % 2) - 1, 0), count - 1)
                far_route.append((start, int(goal[group * count + other])))
        from_far = lax.ppermute(far, axes, far_route)
        from_near = lax.ppermute(near, axes, near_route)
        if later < ROUNDS:
            far, near = pl.pallas_call(
                functools.partial(next_kernel, order, later == ROUNDS - 1),
                out_shape=[shape(BLK, order + (later + 1) * WIDTH)] * 2,
                in_specs=[vmem(), vmem()],
                out_specs=[vmem()] * 2,
                scratch_shapes=[store],
                compiler_params=PARAMS,
                name="next_round",
            )(from_far, from_near)
    work, basis = pl.pallas_call(
        last_kernel,
        out_shape=[shape(order, WIDTH)] * 2,
        in_specs=[vmem(), vmem()],
        out_specs=[hbm()] * 2,
        scratch_shapes=[pltpu.VMEM((order, WIDTH), jnp.float32)] * 2
        + [pltpu.SemaphoreType.DMA((1 + order // CHUNK,))],
        compiler_params=PARAMS,
        name="output",
    )(from_far, from_near)
    return work[None], basis[None]


def solution(mesh):
    return jax.shard_map(
        shards,
        mesh=mesh,
        in_specs=(P(None, ("fac", "jac"), None), P()),
        out_specs=(P("fac", None, "jac"), P("fac", None, "jac")),
        check_vma=False,
    )
```

```python
import functools

import jax
import jax.numpy as jnp
import numpy as np
from jax import lax
from jax.experimental import pallas as pl
from jax.experimental.pallas import tpu as pltpu
from jax.sharding import PartitionSpec as P

ROUNDS = 3
CHUNK = 256
CHAINS = (
    ((0, 1), (0, 0), (1, 3), (1, 2), (2, 1), (2, 0), (3, 3), (3, 2)),
    ((0, 3), (0, 2), (1, 1), (1, 0), (2, 3), (2, 2), (3, 1), (3, 0)),
)
BLK = 64
WIDTH = 2 * BLK
SECTIONS = 16
SUB = 8
GROUPS = SECTIONS // SUB


def lane_ids(rows):
    return lax.broadcasted_iota(jnp.int32, (rows, WIDTH), 1)


def angles(alpha, beta, gamma):
    diff = beta - alpha
    square = diff * diff + 4.0 * gamma * gamma
    inverse = jnp.where(square > 0, lax.rsqrt(square), 0.0)
    along = diff * inverse
    lead = 1.0 + jnp.abs(along)
    cross = (2.0 * gamma) * inverse * along
    scale = lax.rsqrt(lead * lead + cross * cross)
    c, s = lead * scale, cross * scale
    short = (1.0 - c * c) - s * s
    return c + short * (0.5 * c), s + short * (0.5 * s)


def small_rotation(gram, store, swapped):
    lanes = lane_ids(WIDTH)
    rows = lax.broadcasted_iota(jnp.int32, (WIDTH, WIDTH), 0)
    reach = SECTIONS - 1 - (lanes & (SECTIONS - 1))
    skew = ((rows + reach) & (BLK - 1)) + jnp.where((lanes & SECTIONS) == 0, 0, BLK)
    store[...] = jnp.take_along_axis(gram, skew, axis=1).T
    low = lane_ids(SUB) < BLK
    sublane = lax.broadcasted_iota(jnp.int32, (SUB, WIDTH), 0)
    aa, bb, tt, dd = [], [], [], []
    for v in range(GROUPS):
        begin = SECTIONS - SUB * (v + 1)
        top, bot = store[begin:begin + SUB, :], store[SECTIONS + begin:SECTIONS + begin + SUB, :]
        top_swap, bot_swap = pltpu.roll(top, BLK, 1), pltpu.roll(bot, BLK, 1)
        blocks = (
            jnp.where(low, top, top_swap),
            jnp.where(low, bot, bot_swap),
            jnp.where(low, top_swap, top),
            jnp.where(low, bot_swap, bot),
        )
        aa.append(jnp.where(swapped, blocks[3], blocks[0]))
        bb.append(jnp.where(swapped, blocks[2], blocks[1]))
        tt.append(jnp.where(swapped, blocks[1], blocks[2]))
        dd.append(jnp.where(swapped, blocks[0], blocks[3]))
    start = jnp.where(sublane == 0, 1.0, 0.0).astype(jnp.float32)
    zero = jnp.zeros((SUB, WIDTH), jnp.float32)
    ru = [jnp.where(low, start, 0.0)] + [zero] * (GROUPS - 1)
    rl = [jnp.where(low, 0.0, start)] + [zero] * (GROUPS - 1)

    def spread(x, row):
        return jnp.broadcast_to(x[row:row + 1], (SUB, WIDTH))

    alpha, beta, gamma = (spread(x[0], SUB - 1) for x in (aa, dd, bb))
    a_next, b_next, t_next, d_next = (spread(x[0], SUB - 2) for x in (aa, bb, tt, dd))
    for section in range(SECTIONS):
        c, s = angles(alpha, beta, gamma)
        c_up, s_up = pltpu.roll(c, WIDTH - 1, 1), pltpu.roll(s, WIDTH - 1, 1)
        for v in range(section // SUB + 1):
            cc = pltpu.roll(c, SUB * v, 1, stride=1, stride_axis=0)
            ss = pltpu.roll(s, SUB * v, 1, stride=1, stride_axis=0)
            ru[v], rl[v] = cc * ru[v] - ss * rl[v], ss * ru[v] + cc * rl[v]
        if section == SECTIONS - 1:
            break
        moved = [pltpu.roll(x, 1, 0) for x in rl]
        rl = [jnp.where(sublane == 0, before, x) for before, x in zip([zero] + moved[:-1], moved)]
        a1, t1 = c * alpha - s * gamma, c * gamma - s * beta
        new_beta = s * (s * alpha + c * gamma) + c * (s * gamma + c * beta)
        alpha, beta, rest = c * a1 - s * t1, pltpu.roll(new_beta, WIDTH - 1, 1), s * a1 + c * t1
        b1, d1 = s_up * a_next + c_up * b_next, s_up * t_next + c_up * d_next
        gamma = c * b1 - s * d1
        if section == SECTIONS - 2:
            continue
        a1, t1 = c_up * a_next - s_up * b_next, c_up * t_next - s_up * d_next
        a_next = c * a1 - s * t1
        t_next, d_next = pltpu.roll(rest, WIDTH - 1, 1), pltpu.roll(s * b1 + c * d1, WIDTH - 1, 1)
        kept = (SECTIONS - 1 - section) // SUB + 1
        aa, bb, tt, dd = aa[:kept], bb[:kept], tt[:kept], dd[:kept]
        for v in range(kept):
            cc = pltpu.roll(c, BLK - SUB * (v + 1) + 1, 1, stride=1, stride_axis=0)
            ss = pltpu.roll(s, BLK - SUB * (v + 1) + 1, 1, stride=1, stride_axis=0)
            a1, b1 = cc * aa[v] - ss * bb[v], ss * aa[v] + cc * bb[v]
            t1, d1 = cc * tt[v] - ss * dd[v], ss * tt[v] + cc * dd[v]
            b2 = c * b1 - s * d1
            if v == 0:
                b_next = spread(b2, SUB - 3)
            aa[v], bb[v] = c * a1 - s * t1, pltpu.roll(b2, 1, 0)
            tt[v] = pltpu.roll(pltpu.roll(s * a1 + c * t1, WIDTH - 1, 1), SUB - 1, 0)
            dd[v] = pltpu.roll(s * b1 + c * d1, WIDTH - 1, 1)
        bb = [jnp.where(sublane == 0, after, x) for x, after in zip(bb, bb[1:] + [zero])]
        tt = [jnp.where(sublane == SUB - 1, before, x) for before, x in zip([gamma] + tt[:-1], tt)]
    for v in range(GROUPS):
        store[SUB * v:SUB * (v + 1), :] = ru[v]
        store[SECTIONS + SUB * v:SECTIONS + SUB * (v + 1), :] = rl[v]
    upper = (lanes & BLK) == 0
    diagonal = (rows - lanes + jnp.where(upper, 0, SECTIONS - 1)) & (BLK - 1)
    index = (diagonal & (SECTIONS - 1)) + jnp.where(upper, 0, SECTIONS)
    return jnp.where(diagonal < SECTIONS, jnp.take_along_axis(store[...].T, index, axis=1), 0.0)


def deal_kernel(assignment, stats, out, owners, slabs, sems):
    factors, _, order = stats.shape
    count = order // WIDTH
    copies = [pltpu.make_async_copy(stats.at[f], slabs.at[f], sems.at[f]) for f in range(factors)]
    for copy in copies:
        copy.start()
    table = pltpu.make_async_copy(assignment, owners, sems.at[factors])
    table.start()
    table.wait()
    for factor in range(factors):
        group = owners[factor]
        odd = group % 2 == 1
        base = group // 2 * (2 * count)
        copies[factor].wait()
        for place in range(count):
            home = base + jnp.where(odd, home_of(1, place, count), home_of(0, place, count))
            out[home] = slabs[factor, :, place * WIDTH:(place + 1) * WIDTH]


def pieces(x):
    high = x.astype(jnp.bfloat16)
    rest = x - high.astype(jnp.float32)
    middle = rest.astype(jnp.bfloat16)
    low = (rest - middle.astype(jnp.float32)).astype(jnp.bfloat16)
    return high, middle, low


def gram_of(parts, across):
    full = jnp.dot(jnp.concatenate(parts, axis=0), across, preferred_element_type=jnp.float32)
    crossed = full[2 * WIDTH:, :WIDTH]
    small = full[WIDTH:2 * WIDTH, WIDTH:] + (crossed + crossed.T)
    return full[:WIDTH, :WIDTH] + (full[:WIDTH, WIDTH:] + full[WIDTH:2 * WIDTH, :WIDTH] + small)


def apply(rotation, parts, near, far, start, exact):
    high, middle, low = pieces(rotation)
    first = jnp.concatenate(
        [jnp.concatenate([high, middle], axis=1), jnp.concatenate([middle, high], axis=1)], axis=0
    )
    last = jnp.concatenate([low, high], axis=1)
    total = parts[0].shape[1]
    for begin in range(0, total, CHUNK):
        end = min(begin + CHUNK, total)
        part = [x[:, begin:end] for x in parts]
        both = jnp.dot(first, jnp.concatenate(part[:2], axis=0), preferred_element_type=jnp.float32)
        small = both[WIDTH:]
        if exact:
            small = small + jnp.dot(
                last, jnp.concatenate([part[0], part[2]], axis=0), preferred_element_type=jnp.float32
            )
        post(near, far, pl.ds(start + begin, end - begin), both[:WIDTH] + small)


def swap_halves(x, axis, swapped):
    return jnp.where(swapped, pltpu.roll(x, BLK, axis), x)


def place_here():
    cell = lax.axis_index("jac")
    pair = 0
    for chain in CHAINS:
        for number, (x, z) in enumerate(chain):
            pair = jnp.where(cell == 4 * x + z, number, pair)
    return 2 * pair + lax.axis_index("fac") % 2


def leave_rotation(gram, store, place, swapped):
    rotation = small_rotation(gram, store, swapped).T
    bottom_first = jnp.logical_or(place == 0, place % 2 == 1)
    return swap_halves(rotation, 0, bottom_first)


def post(near, far, columns, block):
    near[:, columns] = block[:BLK]
    far[:, columns] = block[BLK:]


def first_kernel(work, far, near, store):
    place = place_here()
    order = work.shape[0]
    straight = work[...]
    parts = pieces(straight.T)
    across = jnp.concatenate(pieces(straight)[:2], axis=1)
    rotation = leave_rotation(gram_of(parts, across), store, place, False)
    apply(rotation, parts, near, far, 0, True)
    post(near, far, pl.ds(order, WIDTH), rotation)


def next_kernel(order, final, from_far, from_near, far, near, store):
    place = place_here()
    swapped = place % 2 == 0
    parts = pieces(jnp.concatenate([from_near[:, :order], from_far[:, :order]], axis=0))
    across = jnp.concatenate(parts[:2], axis=0).T
    rotation = leave_rotation(gram_of(parts, across), store, place, swapped)
    rotation = swap_halves(rotation, 1, swapped)
    apply(rotation, parts, near, far, 0, not final)
    blank = jnp.zeros((BLK, WIDTH), jnp.float32)
    near_basis = [from_near[:, c:c + WIDTH] for c in range(order, from_near.shape[1], WIDTH)]
    far_basis = [from_far[:, c:c + WIDTH] for c in range(order, from_far.shape[1], WIDTH)]
    if final:
        near_basis, far_basis = near_basis + [blank], [far_basis[1], blank, far_basis[0]]
    else:
        near_basis, far_basis = near_basis + [blank], [blank] + far_basis
    columns = [jnp.concatenate(halves, axis=0) for halves in zip(near_basis, far_basis)]
    apply(rotation, pieces(jnp.concatenate(columns, axis=1)), near, far, order, False)


def last_kernel(from_far, from_near, work, basis, work_store, basis_store, sems):
    order = work.shape[0]
    place = lax.axis_index("jac")
    count = lax.axis_size("jac")
    next_chip = far_place(place, count)
    rows = [
        [place ^ 1, next_chip, far_place(place ^ 1, count) ^ 1],
        [next_chip, far_place(next_chip ^ 1, count), far_place(next_chip, count) ^ 1],
    ]
    even = place % 2 == 0
    basis_store[...] = jnp.zeros_like(basis_store)
    chunks = (from_near.shape[1] - order) // WIDTH
    left_half = lane_ids(WIDTH) < BLK
    for chunk in range(chunks):
        columns = pl.ds(order + chunk * WIDTH, WIDTH)
        piece = jnp.concatenate([from_near[:, columns], from_far[:, columns]], axis=0).T
        piece = swap_halves(piece, 1, even)
        for half in range(2):
            row = pl.multiple_of(rows[half][chunk] * WIDTH, WIDTH)
            left = jnp.logical_xor(even, half == 0)
            basis_store[pl.ds(row, WIDTH), :] += jnp.where(left_half == left, piece, 0.0)
    copies = [pltpu.make_async_copy(basis_store, basis, sems.at[0])]
    copies[0].start()
    for number, begin in enumerate(range(0, order, CHUNK)):
        rows = pl.ds(begin, CHUNK)
        near, far = from_near[:, rows], from_far[:, rows]
        pair = [jnp.where(even, far, near), jnp.where(even, near, far)]
        work_store[rows, :] = jnp.concatenate(pair, axis=0).T
        copies.append(pltpu.make_async_copy(work_store.at[rows], work.at[rows], sems.at[number + 1]))
        copies[-1].start()
    for copy in copies:
        copy.wait()


def far_place(place, count):
    return jnp.clip(place + 2 * (place % 2) - 1, 0, count - 1)


def home_of(group, place, count):
    x, z = CHAINS[group % 2][place // 2]
    return (group // 2 * 2 + place % 2) * count + 4 * x + z


def vmem():
    return pl.BlockSpec(memory_space=pltpu.VMEM)


def hbm():
    return pl.BlockSpec(memory_space=pltpu.HBM)


MIB = 1024 * 1024
PARAMS = pltpu.CompilerParams(vmem_limit_bytes=40 * MIB)
DEAL_PARAMS = pltpu.CompilerParams(vmem_limit_bytes=62 * MIB + MIB // 2)


def shape(*dims):
    return jax.ShapeDtypeStruct(dims, jnp.float32)


def shards(statistics, assignment):
    factors, slab, order = statistics.shape
    count = order // WIDTH
    devices = factors * count
    axes = ("fac", "jac")
    home = np.array([home_of(g, p, count) for g in range(factors) for p in range(count)], np.int32)
    dealt = pl.pallas_call(
        deal_kernel,
        out_shape=shape(devices, slab, WIDTH),
        in_specs=[hbm(), hbm()],
        out_specs=vmem(),
        scratch_shapes=[
            pltpu.SMEM((factors,), jnp.int32),
            pltpu.VMEM((factors, slab, order), jnp.float32),
            pltpu.SemaphoreType.DMA((factors + 1,)),
        ],
        compiler_params=DEAL_PARAMS,
        name="deal",
    )(assignment, statistics)
    moved = lax.all_to_all(dealt, axes, split_axis=0, concat_axis=0, tiled=True)
    work = moved.reshape(order, WIDTH)
    store = pltpu.VMEM((WIDTH, WIDTH), jnp.float32)
    far, near = pl.pallas_call(
        first_kernel,
        out_shape=[shape(BLK, order + WIDTH)] * 2,
        in_specs=[vmem()],
        out_specs=[vmem()] * 2,
        scratch_shapes=[store],
        compiler_params=PARAMS,
        name="first_round",
    )(work)
    for later in range(1, ROUNDS + 1):
        goal = home if later < ROUNDS else np.arange(devices, dtype=np.int32)
        near_route, far_route = [], []
        for group in range(factors):
            for place in range(count):
                start = int(home[group * count + place])
                near_route.append((start, int(goal[group * count + (place ^ 1)])))
                other = min(max(place + 2 * (place % 2) - 1, 0), count - 1)
                far_route.append((start, int(goal[group * count + other])))
        from_far = lax.ppermute(far, axes, far_route)
        from_near = lax.ppermute(near, axes, near_route)
        if later < ROUNDS:
            far, near = pl.pallas_call(
                functools.partial(next_kernel, order, later == ROUNDS - 1),
                out_shape=[shape(BLK, order + (later + 1) * WIDTH)] * 2,
                in_specs=[vmem(), vmem()],
                out_specs=[vmem()] * 2,
                scratch_shapes=[store],
                compiler_params=PARAMS,
                name="next_round",
            )(from_far, from_near)
    work, basis = pl.pallas_call(
        last_kernel,
        out_shape=[shape(order, WIDTH)] * 2,
        in_specs=[vmem(), vmem()],
        out_specs=[hbm()] * 2,
        scratch_shapes=[pltpu.VMEM((order, WIDTH), jnp.float32)] * 2
        + [pltpu.SemaphoreType.DMA((1 + order // CHUNK,))],
        compiler_params=PARAMS,
        name="output",
    )(from_far, from_near)
    return work[None], basis[None]


def solution(mesh):
    return jax.shard_map(
        shards,
        mesh=mesh,
        in_specs=(P(None, ("fac", "jac"), None), P()),
        out_specs=(P("fac", None, "jac"), P("fac", None, "jac")),
        check_vma=False,
    )
```
